32 devices in a mesh: blk: 8 (over y, x, core), rows: 4 (over z).
Axes of the slice: x: 2, y: 2, z: 4, core: 2. Of those that a mesh axis runs over, the one named last changes fastest.
Arguments:
- embeddings: bfloat16 [16384, 384], P(('blk', 'rows')), may hold values from -40 to 40
- factors: bfloat16 [8, 384, 384], P('blk'), may hold values from -4 to 4
- centres: bfloat16 [8, 384], P('blk'), may hold values from -3 to 3
- log_prior: bfloat16 [8], P('blk'), may hold values from -1 to 201
Outputs:
- responsibility: float32 [8, 16384], P(None, ('blk', 'rows'))
- counts: float32 [8], replicated
- first_moment: float32 [8, 384], replicated
- second_moment: float32 [8, 384, 384], P('blk')
The draws below stay inside these ranges and needn't reach their ends.
All inputs are finite; a program needn't handle non-finite values.
Results may differ from the reference program's by a relative error of at most 0.0011.
Values may be sent and summed in bfloat16 or wider, within the bound.
No kernel may reach another device: no remote copies, remote signals or barrier semaphores. Data moves between devices by JAX's collectives and lax.ppermute only.
A program may use at most 128 MiB of HBM per device.

```python
import math
import jax
import jax.numpy as jnp
from jax import lax

D = 384
K = 8
ROWS = 16384


def draw_embeddings(key, part):
    subkeys = jax.random.split(jax.random.fold_in(key, 11), 1)
    values = jax.random.normal(subkeys[0], (ROWS, D), jnp.float32)
    values = jnp.clip(values, -6.0, 6.0)
    return values.astype(jnp.bfloat16)


def draw_factors(key, part):
    subkeys = jax.random.split(jax.random.fold_in(key, 23), 2)
    diagonal_part = jnp.exp(jax.random.uniform(subkeys[0], (K, D), jnp.float32, math.log(0.7), math.log(1.4)))
    dense_part = jax.random.normal(subkeys[1], (K, D, D), jnp.float32)
    dense_part = dense_part * (0.5 / math.sqrt(D))
    values = dense_part + diagonal_part[:, :, None] * jnp.eye(D, dtype=jnp.float32)[None, :, :]
    return jnp.clip(values, -4.0, 4.0).astype(jnp.bfloat16)


def draw_log_prior(key, part):
    subkeys = jax.random.split(jax.random.fold_in(key, 37), 1)
    values = jax.random.uniform(subkeys[0], (K,), jnp.float32, -1.0, 1.0)
    return values.astype(jnp.bfloat16)


def block_scale(stream_key, shape, shards, smallest, top_value):
    loudness = 1.0
    for position, parts in shards:
        heights = jax.random.uniform(jax.random.fold_in(jax.random.fold_in(stream_key, 6), position), (parts,), jnp.float32, smallest / len(shards), top_value / len(shards))
        loudness = loudness * jnp.repeat(jnp.exp(heights), shape[position] // parts).reshape((-1,) + (1,) * (len(shape) - 1 - position))
    return loudness


def centred(stream_key, extent, width, reach, cuts=(), kind=jnp.bfloat16):
    gain = block_scale(stream_key, extent, cuts, -0.22, 0.18) if cuts else 1.0
    result = jax.random.normal(stream_key, extent, jnp.float32) * width * gain
    return jnp.minimum(jnp.maximum(result, -reach), reach).astype(kind)


def setup_inputs(seed: int = 0) -> dict:
    key_of = jax.random.split(jax.random.key(seed), 5)
    return {
        "embeddings": draw_embeddings(jax.random.fold_in(key_of[4], 71), 0),
        "factors": draw_factors(jax.random.fold_in(key_of[4], 71), 0),
        "centres": centred(key_of[2], (K, D), 0.5, 3.0, ((0, 8),)),
        "log_prior": draw_log_prior(jax.random.fold_in(key_of[4], 71), 0),
    }


half_temper = 0.05


def reference(embeddings, factors, centres, log_prior):
    def score_one(packed):
        factor_mat, centre_row, prior_val = packed
        whitened = jnp.dot(embeddings, factor_mat, preferred_element_type=jnp.float32) - centre_row.astype(jnp.float32)
        return prior_val.astype(jnp.float32) - half_temper * jnp.sum(whitened * whitened, axis=1)

    scores = lax.map(score_one, (factors, centres, log_prior))
    peak = jnp.max(scores, axis=0, keepdims=True)
    unnorm = jnp.exp(scores - peak)
    responsibility = unnorm / jnp.sum(unnorm, axis=0, keepdims=True)
    normalizer = K / ROWS
    counts = jnp.sum(responsibility, axis=1) * normalizer
    as_float = embeddings.astype(jnp.float32)
    first_moment = jnp.dot(responsibility, as_float, precision=lax.Precision.HIGHEST, preferred_element_type=jnp.float32) * normalizer

    def second_one(resp_row):
        weighted = resp_row[:, None] * as_float
        return jnp.dot(weighted.T, as_float, precision=lax.Precision.HIGHEST, preferred_element_type=jnp.float32) * normalizer

    second_moment = lax.map(second_one, responsibility)
    return responsibility, counts, first_moment, second_moment
```

```python
import jax
import jax.numpy as jnp
from jax import lax
from jax.experimental import pallas as pl
from jax.experimental.pallas import tpu as pltpu
from jax.sharding import PartitionSpec as P

half_temper = 0.05
LANES = 128
TAIL = 16
HEAD = 16
VMEM_LIMIT = 40 * 1024 * 1024
NT = (((1,), (1,)), ((), ()))


def split_two(value):
    high = value.astype(jnp.bfloat16)
    low = (value - high.astype(jnp.float32)).astype(jnp.bfloat16)
    return high, low


def exponent_of(largest):
    bits = jnp.ceil(jnp.log(jnp.maximum(largest, 1e-35)) * 1.4426950408889634) - 12.0
    return jnp.clip(bits, -110.0, 110.0)


def score_kernel(offsets, me_ref, own_ref, near_ref, *refs):
    packs, out_ref = refs[:-1], refs[-1]
    rows, width = own_ref.shape
    me = me_ref[0]
    for offset, pack_ref in zip(offsets, packs, strict=True):
        turned = pack_ref[:width, :].T
        tail = pack_ref[width:, :].astype(jnp.float32)
        centre = tail.T[:, 0:1]
        prior = tail[1:2, 0:1]
        for part, rows_ref in enumerate((own_ref, near_ref)):
            whitened = (
                lax.dot_general(turned, rows_ref[...], NT, preferred_element_type=jnp.float32) - centre
            )
            score = prior - half_temper * jnp.sum(whitened * whitened, axis=0, keepdims=True)
            out_ref[pl.ds(me ^ offset, 1), part * rows : (part + 1) * rows] = score


def softmax(scores):
    peak = jnp.max(scores, axis=0, keepdims=True)
    unnorm = jnp.exp(scores - peak)
    return unnorm / jnp.sum(unnorm, axis=0, keepdims=True)


def moment(resp, component, blocks):
    width = blocks[0].shape[1]
    parts = width // LANES
    total = [0.0] * parts
    for weights, block_ref in zip(resp, blocks, strict=True):
        picked = lax.broadcasted_iota(jnp.int32, weights.shape, 0) == component
        row = jnp.sum(jnp.where(picked, weights, 0.0), axis=0, keepdims=True)
        block = block_ref[...]
        high, low = split_two(block.T.astype(jnp.float32) * row)
        for a in range(parts):
            left = jnp.concatenate(
                [high[a * LANES : (a + 1) * LANES], low[a * LANES : (a + 1) * LANES]], axis=0
            )
            both = jnp.dot(left, block[:, a * LANES :], preferred_element_type=jnp.float32)
            total[a] = total[a] + (both[:LANES] + both[LANES:])
    return total


def store_moment(total, normalizer, out_ref, head):
    largest = jnp.zeros((1, 1), jnp.float32)
    for band in total:
        largest = jnp.maximum(largest, jnp.max(jnp.abs(band[:, :LANES]), keepdims=True))
    exponent = exponent_of(largest * normalizer)
    factor = normalizer * jnp.exp2(-exponent)
    at = 0
    for band in total:
        for b in range(band.shape[1] // LANES):
            out_ref[at : at + LANES, :] = band[:, b * LANES : (b + 1) * LANES] * factor
            at += LANES
    out_ref[head : head + 1, :] = jnp.broadcast_to(exponent, (1, LANES))


def give_kernel(offsets, normalizer, me_ref, own_s, near_s, core_s, far_s, *refs):
    blocks, (resp_ref, low_ref), outs = refs[:4], refs[4:6], refs[6:]
    comps, rows = resp_ref.shape[0], blocks[0].shape[0]
    width = blocks[0].shape[1]
    me = me_ref[0]
    index = lax.broadcasted_iota(jnp.int32, (comps, rows), 0)
    mine = ((index ^ me) & 2) == 0
    resp = []
    for here, there in ((own_s, near_s), (core_s, far_s)):
        resp.append(softmax(jnp.where(mine, here[:, :rows], there[:, rows:])))
        resp.append(softmax(jnp.where(mine, here[:, rows:], there[:, :rows])))
    for part, weights in enumerate(resp):
        resp_ref[:, part * rows : (part + 1) * rows] = weights
    for offset, out_ref in zip(offsets, outs, strict=True):
        store_moment(moment(resp, me ^ offset, blocks), normalizer, out_ref, out_ref.shape[0] - HEAD)
    firsts, counts = [], []
    for weights, block_ref in zip(resp, blocks, strict=True):
        high = weights.astype(jnp.bfloat16).astype(jnp.float32)
        rest = weights - high
        middle = rest.astype(jnp.bfloat16).astype(jnp.float32)
        stacked = jnp.concatenate([high, middle, rest - middle], axis=0).astype(jnp.bfloat16)
        product = jnp.dot(stacked, block_ref[...], preferred_element_type=jnp.float32)
        firsts.append(product[:comps] + (product[comps : 2 * comps] + product[2 * comps :]))
        counts.append(jnp.sum(weights, axis=1, keepdims=True))
    first = ((firsts[0] + firsts[2]) + (firsts[1] + firsts[3])) * normalizer
    count = ((counts[0] + counts[2]) + (counts[1] + counts[3])) * normalizer
    exponent = exponent_of(jnp.max(jnp.abs(first), keepdims=True))
    first = first * jnp.exp2(-exponent)
    parts = width // LANES
    for a in range(parts):
        low_ref[a * comps : (a + 1) * comps, :] = first[:, a * LANES : (a + 1) * LANES]
    low_ref[parts * comps : (parts + 1) * comps, :] = jnp.broadcast_to(count, (comps, LANES))
    low_ref[(parts + 1) * comps :, :] = jnp.broadcast_to(exponent, (HEAD, LANES))
    for out_ref in outs:
        end = out_ref.shape[0]
        start = end - low_ref.shape[0]
        out_ref[start : end - HEAD, :] = low_ref[: (parts + 1) * comps, :]
        out_ref[end - HEAD + 1 :, :] = low_ref[(parts + 1) * comps + 1 :, :]


def keep_kernel(normalizer, me_ref, resp_ref, low_ref, *refs):
    blocks, (out_ref, here_ref) = refs[:4], refs[4:]
    rows = blocks[0].shape[0]
    resp = [resp_ref[:, part * rows : (part + 1) * rows] for part in range(4)]
    end = out_ref.shape[0]
    start = end - low_ref.shape[0]
    out_ref[start:, :] = low_ref[...]
    store_moment(moment(resp, me_ref[0], blocks), normalizer, out_ref, end - HEAD)
    here_ref[...] = resp_ref[:, :rows]


def unpack_kernel(packed_ref, second_ref, first_ref, count_ref):
    width = second_ref.shape[1]
    comps = first_ref.shape[0]
    parts = width // LANES
    at = 0
    for a in range(parts):
        for b in range(a, parts):
            block = packed_ref[at : at + LANES, :]
            second_ref[a * LANES : (a + 1) * LANES, b * LANES : (b + 1) * LANES] = block
            if b > a:
                second_ref[b * LANES : (b + 1) * LANES, a * LANES : (a + 1) * LANES] = block.T
            at += LANES
    for a in range(parts):
        first_ref[:, a * LANES : (a + 1) * LANES] = packed_ref[at : at + comps, :]
        at += comps
    count_ref[...] = packed_ref[at : at + comps, :].T[0:1, :]


def tree(values):
    while len(values) > 1:
        values = [values[i] + values[i + 1] for i in range(0, len(values), 2)]
    return values[0]


def combine(messages, second_rows, first_rows, encode):
    height = messages[0].shape[0]
    head = height - HEAD
    row = lax.broadcasted_iota(jnp.int32, messages[0].shape, 0)
    wide = [m.astype(jnp.float32) for m in messages]

    def at_rows(second, first, other):
        return jnp.where(row < second_rows, second, jnp.where(row < second_rows + first_rows, first, other))

    seconds = [w[head : head + 1] for w in wide]
    firsts = [w[head + 1 : head + 2] for w in wide]
    total = tree([w * at_rows(jnp.exp2(s), jnp.exp2(f), 1.0) for w, s, f in zip(wide, seconds, firsts, strict=True)])
    if not encode:
        return total
    grow = float((len(messages) - 1).bit_length())
    second, first = seconds[0], firsts[0]
    for s, f in zip(seconds[1:], firsts[1:], strict=True):
        second, first = jnp.maximum(second, s), jnp.maximum(first, f)
    second, first = second + grow, first + grow
    scaled = total * at_rows(jnp.exp2(-second), jnp.exp2(-first), 1.0)
    scaled = jnp.where(row < head, scaled, jnp.where(row == head, second, first))
    return scaled.astype(jnp.float16)


def call(kernel, out_shape, args, flops, smem_first=True):
    specs = [pl.BlockSpec(memory_space=pltpu.VMEM)] * len(args)
    if smem_first:
        specs[0] = pl.BlockSpec(memory_space=pltpu.SMEM)
    moved = sum(a.size * a.dtype.itemsize for a in args) + sum(
        o.size * o.dtype.itemsize for o in jax.tree.leaves(out_shape)
    )
    return pl.pallas_call(
        kernel,
        out_shape=out_shape,
        in_specs=specs,
        out_specs=jax.tree.map(lambda _: pl.BlockSpec(memory_space=pltpu.VMEM), out_shape),
        compiler_params=pltpu.CompilerParams(vmem_limit_bytes=VMEM_LIMIT),
        cost_estimate=pl.CostEstimate(flops=flops, bytes_accessed=moved, transcendentals=0),
    )(*args)


def solution(mesh):
    n_blk, n_rows = mesh.shape["blk"], mesh.shape["rows"]
    groups = n_blk // 4

    def hop(value, blk, rows):
        if rows == 0:
            return lax.ppermute(value, "blk", [(i, i ^ blk) for i in range(n_blk)])
        if blk == 0:
            return lax.ppermute(value, "rows", [(i, i ^ rows) for i in range(n_rows)])
        pairs = [
            (i * n_rows + j, (i ^ blk) * n_rows + (j ^ rows)) for i in range(n_blk) for j in range(n_rows)
        ]
        return lax.ppermute(value, ("blk", "rows"), pairs)

    def shards(embeddings, factors, centres, log_prior):
        rows, width = embeddings.shape
        comps = factors.shape[0] * n_blk
        normalizer = comps / (rows * n_blk * n_rows)
        parts = width // LANES
        second_rows = parts * (parts + 1) // 2 * LANES
        first_rows = parts * comps
        low_rows = first_rows + comps + HEAD
        height = second_rows + low_rows
        me = lax.axis_index("blk").astype(jnp.int32).reshape(1)

        near = hop(embeddings, 2, 0)
        pack = jnp.concatenate(
            [
                factors.reshape(width, width),
                centres,
                jnp.broadcast_to(log_prior[:, None], (1, width)),
                jnp.zeros((TAIL - 2, width), jnp.bfloat16),
            ],
            axis=0,
        )
        packs = [pack] + [hop(pack, 4 * b, 0) for b in range(1, groups)]
        core = hop(embeddings, 1, 0)
        packs = [p for q in packs for p in (q, hop(q, 1, 0))]
        offsets = [4 * b + c for b in range(groups) for c in range(2)]

        scores = call(
            lambda *refs: score_kernel(offsets, *refs),
            jax.ShapeDtypeStruct((comps, 2 * rows), jnp.float32),
            (me, embeddings, near, *packs),
            2 * len(offsets) * 2 * rows * width * width,
        )
        near_scores = hop(scores, 2, 0)
        core_scores = hop(scores, 1, 0)
        far = hop(near, 1, 0)
        far_scores = hop(near_scores, 1, 0)

        blocks = (embeddings, near, core, far)
        message = jax.ShapeDtypeStruct((height, LANES), jnp.float32)
        flops = 4 * 4 * rows * width * width
        resp, low, *given = call(
            lambda *refs: give_kernel([4 * b for b in range(1, groups)], normalizer, *refs),
            (
                jax.ShapeDtypeStruct((comps, 4 * rows), jnp.float32),
                jax.ShapeDtypeStruct((low_rows, LANES), jnp.float32),
                *[message] * (groups - 1),
            ),
            (me, scores, near_scores, core_scores, far_scores, *blocks),
            flops * (groups - 1),
        )
        given = [g.astype(jnp.float16) for g in given]
        received = {}
        for b in range(1, groups):
            received[b, 1] = hop(given[b - 1], 4 * b, 1)
            received[b, 0] = hop(given[b - 1], 4 * b, 0)
        kept, here = call(
            lambda *refs: keep_kernel(normalizer, *refs),
            (message, jax.ShapeDtypeStruct((comps, rows), jnp.float32)),
            (me, resp, low, *blocks),
            flops,
        )
        received[0, 0] = kept.astype(jnp.float16)
        received[0, 1] = hop(received[0, 0], 0, 1)
        messages = [received[b, z] for b in range(groups) for z in range(2)]
        bit = 2
        while bit < n_rows:
            summed = combine(messages, second_rows, first_rows, True)
            messages = [summed, hop(summed, 0, bit)]
            bit *= 2
        packed = combine(messages, second_rows, first_rows, False)
        second, first, count = call(
            unpack_kernel,
            (
                jax.ShapeDtypeStruct((width, width), jnp.float32),
                jax.ShapeDtypeStruct((comps, width), jnp.float32),
                jax.ShapeDtypeStruct((1, comps), jnp.float32),
            ),
            (packed,),
            0,
            smem_first=False,
        )
        return here, count.reshape(comps), first, second.reshape(1, width, width)

    in_specs = (P(("blk", "rows"), None), P("blk", None, None), P("blk", None), P("blk"))
    out_specs = (P(None, ("blk", "rows")), P(), P(), P("blk", None, None))
    return jax.shard_map(shards, mesh=mesh, in_specs=in_specs, out_specs=out_specs, check_vma=False)
```

```python
import jax
import jax.numpy as jnp
from jax import lax
from jax.experimental import pallas as pl
from jax.experimental.pallas import tpu as pltpu
from jax.sharding import PartitionSpec as P

half_temper = 0.05
LANES = 128
TAIL = 16
EARLY_COST = 0
HEAD = 8
VMEM_LIMIT = 40 * 1024 * 1024
NT = (((1,), (1,)), ((), ()))


def split_two(value):
    high = value.astype(jnp.bfloat16)
    low = (value - high.astype(jnp.float32)).astype(jnp.bfloat16)
    return high, low


def power(exponent):
    whole = exponent.astype(jnp.int32)
    size = jnp.abs(whole)
    result = jnp.ones(exponent.shape, jnp.float32)
    for bit in range(7):
        factor = jnp.where(whole < 0, 0.5 ** (1 << bit), 2.0 ** (1 << bit))
        result = result * jnp.where((size >> bit) & 1 == 1, factor, 1.0)
    return result


def exponent_of(largest):
    bits = jnp.ceil(jnp.log(jnp.maximum(largest, 1e-35)) * 1.4426950408889634) - 12.0
    return jnp.clip(bits, -110.0, 110.0)


def score_rows(turned, tail, rows_ref):
    whitened = lax.dot_general(turned, rows_ref[...], NT, preferred_element_type=jnp.float32)
    whitened = whitened - tail.T[:, 0:1]
    return tail[1:2, 0:1] - half_temper * jnp.sum(whitened * whitened, axis=0, keepdims=True)


def own_kernel(own_ref, core_ref, matrix_ref, tail_ref, out_ref, turned_ref):
    rows = own_ref.shape[0]
    turned_ref[...] = matrix_ref[...].T
    tail = tail_ref[...].astype(jnp.float32)
    for part, rows_ref in enumerate((own_ref, core_ref)):
        out_ref[:, part * rows : (part + 1) * rows] = score_rows(turned_ref[...], tail, rows_ref)


def near_kernel(groups, own_ref, near_ref, core_ref, done_ref, turned_ref, *refs):
    tails, matrices, (out_ref, others_ref) = refs[:groups], refs[groups : 2 * groups - 1], refs[2 * groups - 1 :]
    rows = own_ref.shape[0]
    for b in range(groups):
        if b:
            others_ref[b - 1] = matrices[b - 1][...].T
        turned = others_ref[b - 1] if b else turned_ref[...]
        tail = tails[b][...].astype(jnp.float32)
        for part, rows_ref in enumerate((own_ref, near_ref, core_ref)):
            if b == 0 and part != 1:
                line = done_ref[:, part // 2 * rows : (part // 2 + 1) * rows]
            else:
                line = score_rows(turned, tail, rows_ref)
            out_ref[b : b + 1, part * rows : (part + 1) * rows] = line


def far_kernel(groups, far_ref, done_ref, turned_ref, others_ref, *refs):
    tails, out_ref = refs[:groups], refs[groups]
    rows = far_ref.shape[0]
    out_ref[:, : 3 * rows] = done_ref[...]
    for b in range(groups):
        tail = tails[b][...].astype(jnp.float32)
        turned = others_ref[b - 1] if b else turned_ref[...]
        out_ref[b : b + 1, 3 * rows :] = score_rows(turned, tail, far_ref)


def softmax(scores):
    peak = jnp.max(scores, axis=0, keepdims=True)
    unnorm = jnp.exp(scores - peak)
    return unnorm / jnp.sum(unnorm, axis=0, keepdims=True)


def moment(resp, component, blocks, extra=None):
    width = blocks[0].shape[1]
    parts = width // LANES
    total = [0.0] * parts
    products = []
    for at, (weights, block_ref) in enumerate(zip(resp, blocks, strict=True)):
        picked = lax.broadcasted_iota(jnp.int32, weights.shape, 0) == component
        row = jnp.sum(jnp.where(picked, weights, 0.0), axis=0, keepdims=True)
        block = block_ref[...]
        high, low = split_two(block.T.astype(jnp.float32) * row)
        for a in range(parts):
            left = [high[a * LANES : (a + 1) * LANES], low[a * LANES : (a + 1) * LANES]]
            if a == 0 and extra is not None:
                left.append(extra[at])
            left = jnp.concatenate(left, axis=0)
            both = jnp.dot(left, block[:, a * LANES :], preferred_element_type=jnp.float32)
            total[a] = total[a] + (both[:LANES] + both[LANES : 2 * LANES])
            if a == 0:
                products.append(both[2 * LANES :])
    return total, products


def pair_masks():
    i = lax.broadcasted_iota(jnp.int32, (LANES, LANES), 0)
    j = lax.broadcasted_iota(jnp.int32, (LANES, LANES), 1)
    return i, j


class Layout:
    def __init__(self, width, comps):
        self.parts = width // LANES
        self.comps = comps
        off = self.parts * (self.parts - 1) // 2 * LANES
        folded = self.parts // 2 * LANES + self.parts % 2 * (LANES // 2)
        self.diagonals = off + folded
        self.firsts = self.diagonals + -(-self.parts // 8) * 8
        self.counts = self.firsts + self.parts * comps
        self.half = -(-(self.counts + comps) // 16) * 8
        self.rows = self.half + HEAD

    def write(self, out_ref, flip, at, value):
        done = 0
        while done < value.shape[0]:
            side, row = divmod(at + done, self.half)
            count = min(value.shape[0] - done, self.half - row)
            out_ref[side ^ flip, row : row + count, :] = value[done : done + count]
            done += count


def store_second(total, normalizer, layout, out_ref, flip):
    parts = layout.parts
    largest = jnp.zeros((1, 1), jnp.float32)
    for band in total:
        largest = jnp.maximum(largest, jnp.max(jnp.abs(band[:, :LANES]), keepdims=True))
    exponent = exponent_of(largest * normalizer)
    factor = normalizer * power(-exponent)
    i, j = pair_masks()
    at = 0
    for a in range(parts):
        for b in range(a + 1, parts):
            block = total[a][:, (b - a) * LANES : (b - a + 1) * LANES]
            layout.write(out_ref, flip, at, block * factor)
            at += LANES
    diagonal = [band[:, :LANES] * factor for band in total]
    for a in range(0, parts - 1, 2):
        layout.write(out_ref, flip, at, jnp.where(i <= j, diagonal[a], diagonal[a + 1]))
        at += LANES
    if parts % 2:
        half = LANES // 2
        lower = pltpu.roll(diagonal[-1][half:], half, 1)
        layout.write(out_ref, flip, at, jnp.where(i <= j, diagonal[-1], 0.0)[:half] + jnp.where((i > j)[:half], lower, 0.0))
        at += half
    lines = [jnp.sum(jnp.where(i == j, d, 0.0), axis=0, keepdims=True) for d in diagonal]
    lines += [jnp.zeros((1, LANES), jnp.float32)] * (layout.firsts - at - parts)
    layout.write(out_ref, flip, at, jnp.concatenate(lines, axis=0))
    for side in range(2):
        out_ref[side, layout.half : layout.half + 1, :] = jnp.broadcast_to(exponent, (1, LANES))


def store_low(low_ref, layout, out_ref, flip):
    body = low_ref.shape[0] - HEAD
    layout.write(out_ref, flip, layout.firsts, low_ref[:body, :])
    for side in range(2):
        out_ref[side, layout.half + 1 :, :] = low_ref[body + 1 :, :]


def give_kernel(offsets, normalizer, layout, me_ref, *refs):
    scores, blocks = refs[:4], refs[4:8]
    outs, table_ref = refs[8:-1], refs[-1]
    resp_ref, low_ref, here_ref, *outs = outs
    comps, rows = here_ref.shape
    me, flip = me_ref[0], me_ref[1]
    for source, score_ref in enumerate(scores):
        for b in range(score_ref.shape[0]):
            for part in range(4):
                to = part ^ (((source & 1) << 1) | (source >> 1))
                table_ref[pl.ds(me ^ (4 * b + source), 1), to * rows : (to + 1) * rows] = score_ref[
                    b : b + 1, part * rows : (part + 1) * rows
                ]
    weights = softmax(table_ref[...])
    resp_ref[...] = weights
    here_ref[...] = weights[:, :rows]
    resp = [weights[:, part * rows : (part + 1) * rows] for part in range(4)]
    stacked, counts = [], []
    for weights in resp:
        high = weights.astype(jnp.bfloat16).astype(jnp.float32)
        rest = weights - high
        middle = rest.astype(jnp.bfloat16).astype(jnp.float32)
        pieces = [high, middle, rest - middle]
        if 3 * comps % 16:
            pieces.append(jnp.zeros((-3 * comps % 16, rows), jnp.float32))
        stacked.append(jnp.concatenate(pieces, axis=0).astype(jnp.bfloat16))
        counts.append(jnp.sum(weights, axis=1, keepdims=True))
    totals, products = [], []
    for at, offset in enumerate(offsets):
        total, product = moment(resp, me ^ offset, blocks, stacked if at == 0 else None)
        totals.append(total)
        products = products or product
    firsts = [p[:comps] + (p[comps : 2 * comps] + p[2 * comps : 3 * comps]) for p in products]
    first = ((firsts[0] + firsts[2]) + (firsts[1] + firsts[3])) * normalizer
    count = ((counts[0] + counts[2]) + (counts[1] + counts[3])) * normalizer
    exponent = exponent_of(jnp.max(jnp.abs(first), keepdims=True))
    first = first * power(-exponent)
    body = low_ref.shape[0] - HEAD
    low_ref[...] = jnp.zeros_like(low_ref)
    for a in range(layout.parts):
        low_ref[a * comps : (a + 1) * comps, :] = first[:, a * LANES : (a + 1) * LANES]
    at = layout.parts * comps
    low_ref[at : at + comps, :] = jnp.broadcast_to(count, (comps, LANES))
    low_ref[body:, :] = jnp.broadcast_to(exponent, (HEAD, LANES))
    for total, out_ref in zip(totals, outs, strict=True):
        store_second(total, normalizer, layout, out_ref, flip)
        store_low(low_ref, layout, out_ref, flip)


def keep_kernel(normalizer, layout, me_ref, resp_ref, low_ref, *refs):
    blocks, out_ref = refs[:4], refs[4]
    rows = blocks[0].shape[0]
    resp = [resp_ref[:, part * rows : (part + 1) * rows] for part in range(4)]
    flip = me_ref[1]
    store_second(moment(resp, me_ref[0], blocks)[0], normalizer, layout, out_ref, flip)
    store_low(low_ref, layout, out_ref, flip)


def tree(values):
    while len(values) > 1:
        values = [values[i] + values[i + 1] for i in range(0, len(values), 2)]
    return values[0]


def decoded_sum(refs, side, layout):
    row = lax.broadcasted_iota(jnp.int32, (layout.half, LANES), 0) + side * layout.half
    is_second, is_first = row < layout.firsts, row < layout.counts

    def at_rows(second, first):
        return jnp.where(is_second, power(second), jnp.where(is_first, power(first), 1.0))

    seconds = [r[layout.half : layout.half + 1, :] for r in refs]
    firsts = [r[layout.half + 1 : layout.half + 2, :] for r in refs]
    total = tree([r[: layout.half, :] * at_rows(s, f) for r, s, f in zip(refs, seconds, firsts, strict=True)])
    return total, seconds, firsts, at_rows


def highest(values):
    return values[0] if len(values) == 1 else jnp.maximum(values[0], highest(values[1:]))


def early_kernel(layout, count, me_ref, *refs):
    refs, out_ref = refs[:-1], refs[-1]
    total, _, _, _ = decoded_sum(refs[:count], me_ref[1], layout)
    out_ref[: layout.half, :] = total
    for line in range(2):
        out_ref[layout.half + line : layout.half + line + 1, :] = highest(
            [r[layout.half + line : layout.half + line + 1, :] for r in refs]
        )
    out_ref[layout.half + 2 :, :] = jnp.zeros((HEAD - 2, LANES), jnp.float32)


def combine_kernel(layout, early, me_ref, *refs):
    refs, out_ref = refs[:-1], refs[-1]
    total, seconds, firsts, at_rows = decoded_sum(refs[early:], me_ref[1], layout)
    if early:
        total = refs[0][: layout.half, :] + total
        seconds.append(refs[0][layout.half : layout.half + 1, :])
        firsts.append(refs[0][layout.half + 1 : layout.half + 2, :])
    grow = float((2 * len(refs) - 1).bit_length())
    second, first = highest(seconds) + grow, highest(firsts) + grow
    out_ref[: layout.half, :] = total * at_rows(-second, -first)
    out_ref[layout.half :, :] = jnp.broadcast_to(first, (HEAD, LANES))
    out_ref[layout.half : layout.half + 1, :] = second


def finish_kernel(layout, count, me_ref, *refs):
    mine, others = refs[:count], refs[count : 2 * count]
    second_ref, first_ref, count_ref, table_ref = refs[2 * count :]
    side = me_ref[1]
    for part, messages in ((0, mine), (1, others)):
        total, _, _, _ = decoded_sum(messages, side ^ part, layout)
        table_ref[pl.ds(pl.multiple_of((side ^ part) * layout.half, 8), layout.half), :] = total
    parts, comps = layout.parts, layout.comps
    i, j = pair_masks()

    def place(a, b, block):
        second_ref[a * LANES : (a + 1) * LANES, b * LANES : (b + 1) * LANES] = block

    at = 0
    for a in range(parts):
        for b in range(a + 1, parts):
            block = table_ref[at : at + LANES, :]
            place(a, b, block)
            place(b, a, block.T)
            at += LANES
    lines = [table_ref[layout.diagonals + a : layout.diagonals + a + 1, :] for a in range(parts)]
    for a in range(0, parts - 1, 2):
        block = table_ref[at : at + LANES, :]
        turned = block.T
        place(a, a, jnp.where(i <= j, block, turned))
        place(a + 1, a + 1, jnp.where(i == j, lines[a + 1], jnp.where(i > j, block, turned)))
        at += LANES
    if parts % 2:
        half = LANES // 2
        block = table_ref[at : at + half, :]
        upper = jnp.where((i <= j)[:half], block, 0.0)
        lower = pltpu.roll(jnp.where((i > j)[:half], block, 0.0), half, 1)
        whole = jnp.concatenate([upper, lower], axis=0)
        place(parts - 1, parts - 1, jnp.where(i == j, lines[-1], whole + whole.T))
    at = layout.firsts
    for a in range(parts):
        first_ref[:, a * LANES : (a + 1) * LANES] = table_ref[at : at + comps, :]
        at += comps
    count_ref[...] = table_ref[at : at + comps, :].T[0:1, :]


def call(kernel, out_shape, args, flops, scratch=()):
    specs = [pl.BlockSpec(memory_space=pltpu.VMEM)] * len(args)
    if args[0].dtype == jnp.int32:
        specs[0] = pl.BlockSpec(memory_space=pltpu.SMEM)
    moved = sum(a.size * a.dtype.itemsize for a in args) + sum(
        o.size * o.dtype.itemsize for o in jax.tree.leaves(out_shape)
    )
    return pl.pallas_call(
        kernel,
        out_shape=out_shape,
        in_specs=specs,
        out_specs=jax.tree.map(lambda _: pl.BlockSpec(memory_space=pltpu.VMEM), out_shape),
        scratch_shapes=list(scratch),
        compiler_params=pltpu.CompilerParams(vmem_limit_bytes=VMEM_LIMIT),
        cost_estimate=pl.CostEstimate(flops=flops, bytes_accessed=moved, transcendentals=0),
    )(*args)


def solution(mesh):
    n_blk, n_rows = mesh.shape["blk"], mesh.shape["rows"]
    groups = n_blk // 4

    def hop(value, blk, rows):
        if rows == 0:
            return lax.ppermute(value, "blk", [(i, i ^ blk) for i in range(n_blk)])
        if blk == 0:
            return lax.ppermute(value, "rows", [(i, i ^ rows) for i in range(n_rows)])
        pairs = [
            (i * n_rows + j, (i ^ blk) * n_rows + (j ^ rows)) for i in range(n_blk) for j in range(n_rows)
        ]
        return lax.ppermute(value, ("blk", "rows"), pairs)

    def shards(embeddings, factors, centres, log_prior):
        rows, width = embeddings.shape
        comps = factors.shape[0] * n_blk
        normalizer = comps / (rows * n_blk * n_rows)
        layout = Layout(width, comps)
        low_rows = 2 * layout.half - layout.firsts + HEAD
        me = jnp.stack([lax.axis_index("blk"), lax.axis_index("rows") & 1]).astype(jnp.int32)

        near = hop(embeddings, 2, 0)
        matrix = factors.reshape(width, width)
        tail = jnp.concatenate(
            [
                centres,
                jnp.broadcast_to(log_prior[:, None], (1, width)),
                jnp.zeros((TAIL - 2, width), jnp.bfloat16),
            ],
            axis=0,
        )
        core = hop(embeddings, 1, 0)
        matrices = [hop(matrix, 4 * b, 0) for b in range(1, groups)]
        tails = [hop(tail, 4 * b, 0) for b in range(1, groups)]
        flops = 2 * rows * width * width
        line = lambda count, lanes: jax.ShapeDtypeStruct((count, lanes * rows), jnp.float32)
        turned = jax.ShapeDtypeStruct((width, width), jnp.bfloat16)
        own_scores, own_turned = call(
            own_kernel, (line(1, 2), turned), (embeddings, core, matrix, tail), 2 * flops
        )
        near, matrices, tails, own_scores = lax.optimization_barrier((near, matrices, tails, own_scores))
        far = hop(near, 1, 0)
        blocks = (embeddings, near, core, far)
        tails = [tail] + tails
        most_scores, other_turned = call(
            lambda *refs: near_kernel(groups, *refs),
            (line(groups, 3), jax.ShapeDtypeStruct((groups - 1, width, width), jnp.bfloat16)),
            (embeddings, near, core, own_scores, own_turned, *tails, *matrices),
            (3 * groups - 2) * flops,
        )
        scores = call(
            lambda *refs: far_kernel(groups, *refs),
            line(groups, 4),
            (far, most_scores, own_turned, other_turned, *tails),
            groups * flops,
        )
        near_scores = hop(scores, 2, 0)
        core_scores = hop(scores, 1, 0)
        far_scores = hop(near_scores, 1, 0)

        sent = jax.ShapeDtypeStruct((layout.rows, LANES), jnp.float32)
        message = jax.ShapeDtypeStruct((2, layout.rows, LANES), jnp.float32)
        flops = 4 * 4 * rows * width * width
        resp, low, here, *given = call(
            lambda *refs: give_kernel([4 * b for b in range(1, groups)], normalizer, layout, *refs),
            (
                jax.ShapeDtypeStruct((comps, 4 * rows), jnp.float32),
                jax.ShapeDtypeStruct((low_rows, LANES), jnp.float32),
                jax.ShapeDtypeStruct((comps, rows), jnp.float32),
                *[message] * (groups - 1),
            ),
            (me, scores, core_scores, near_scores, far_scores, *blocks),
            flops * (groups - 1),
            [pltpu.VMEM((comps, 4 * rows), jnp.float32)],
        )
        received = {}
        for b in range(1, groups):
            for z in (1, 0):
                received[b, z] = hop(given[b - 1][z].astype(jnp.float16), 4 * b, z)
        kept = call(
            lambda *refs: keep_kernel(normalizer, layout, *refs),
            message,
            (me, resp, low, *blocks),
            flops,
        )
        received[0, 0] = lax.optimization_barrier(kept[0].astype(jnp.float16))
        received[0, 1] = hop(kept[1].astype(jnp.float16), 0, 1)
        wide = {key: value.astype(jnp.float32) for key, value in received.items()}
        same = [wide[b, 0] for b in range(groups)]
        other = [wide[b, 1] for b in range(1, groups)]
        early = call(
            lambda *refs: early_kernel(layout, groups, *refs), sent, (me, *same, *other), EARLY_COST
        )
        summed = call(
            lambda *refs: combine_kernel(layout, 1, *refs), sent, (me, early, wide[0, 1], *other), 0
        )
        summed = lax.optimization_barrier(summed.astype(jnp.float16))
        bit = 2
        while 2 * bit < n_rows:
            messages = [m.astype(jnp.float32) for m in (summed, hop(summed, 0, bit))]
            summed = call(
                lambda *refs: combine_kernel(layout, 0, *refs), sent, (me, *messages), 0
            )
            summed = lax.optimization_barrier(summed.astype(jnp.float16))
            bit *= 2
        last = [0, bit] if bit < n_rows else [0]
        others = [hop(summed, 0, 1 ^ z) for z in reversed(last)][::-1]
        mine = [summed] + [hop(summed, 0, z) for z in last[1:]]
        second, first, count = call(
            lambda *refs: finish_kernel(layout, len(last), *refs),
            (
                jax.ShapeDtypeStruct((width, width), jnp.float32),
                jax.ShapeDtypeStruct((comps, width), jnp.float32),
                jax.ShapeDtypeStruct((1, comps), jnp.float32),
            ),
            (me, *[m.astype(jnp.float32) for m in mine + others]),
            0,
            [pltpu.VMEM((2 * layout.half, LANES), jnp.float32)],
        )
        return here, count.reshape(comps), first, second.reshape(1, width, width)

    in_specs = (P(("blk", "rows"), None), P("blk", None, None), P("blk", None), P("blk"))
    out_specs = (P(None, ("blk", "rows")), P(), P(), P("blk", None, None))
    return jax.shard_map(shards, mesh=mesh, in_specs=in_specs, out_specs=out_specs, check_vma=False)
```

```python
import jax
import jax.numpy as jnp
from jax import lax
from jax.experimental import pallas as pl
from jax.experimental.pallas import tpu as pltpu
from jax.sharding import PartitionSpec as P

half_temper = 0.05
LANES = 128
TAIL = 16
HEAD = 8
VMEM_LIMIT = 40 * 1024 * 1024
NT = (((1,), (1,)), ((), ()))


def split_two(value):
    high = value.astype(jnp.bfloat16)
    low = (value - high.astype(jnp.float32)).astype(jnp.bfloat16)
    return high, low


def power(exponent):
    whole = exponent.astype(jnp.int32)
    size = jnp.abs(whole)
    result = jnp.ones(exponent.shape, jnp.float32)
    for bit in range(7):
        factor = jnp.where(whole < 0, 0.5 ** (1 << bit), 2.0 ** (1 << bit))
        result = result * jnp.where((size >> bit) & 1 == 1, factor, 1.0)
    return result


def exponent_of(largest):
    bits = jnp.ceil(jnp.log(jnp.maximum(largest, 1e-35)) * 1.4426950408889634) - 12.0
    return jnp.clip(bits, -110.0, 110.0)


def score_rows(turned, tail, rows_ref):
    whitened = lax.dot_general(turned, rows_ref[...], NT, preferred_element_type=jnp.float32)
    whitened = whitened - tail.T[:, 0:1]
    return tail[1:2, 0:1] - half_temper * jnp.sum(whitened * whitened, axis=0, keepdims=True)


def own_kernel(own_ref, core_ref, matrix_ref, tail_ref, out_ref, turned_ref):
    rows = own_ref.shape[0]
    turned_ref[...] = matrix_ref[...].T
    tail = tail_ref[...].astype(jnp.float32)
    for part, rows_ref in enumerate((own_ref, core_ref)):
        out_ref[:, part * rows : (part + 1) * rows] = score_rows(turned_ref[...], tail, rows_ref)


def near_kernel(groups, own_ref, near_ref, core_ref, done_ref, turned_ref, *refs):
    tails, matrices, (out_ref, others_ref) = refs[:groups], refs[groups : 2 * groups - 1], refs[2 * groups - 1 :]
    rows = own_ref.shape[0]
    for b in range(groups):
        if b:
            others_ref[b - 1] = matrices[b - 1][...].T
        turned = others_ref[b - 1] if b else turned_ref[...]
        tail = tails[b][...].astype(jnp.float32)
        for part, rows_ref in enumerate((own_ref, near_ref, core_ref)):
            if b == 0 and part != 1:
                line = done_ref[:, part // 2 * rows : (part // 2 + 1) * rows]
            else:
                line = score_rows(turned, tail, rows_ref)
            out_ref[b : b + 1, part * rows : (part + 1) * rows] = line


def far_kernel(groups, far_ref, done_ref, turned_ref, others_ref, *refs):
    tails, out_ref = refs[:groups], refs[groups]
    rows = far_ref.shape[0]
    out_ref[:, : 3 * rows] = done_ref[...]
    for b in range(groups):
        tail = tails[b][...].astype(jnp.float32)
        turned = others_ref[b - 1] if b else turned_ref[...]
        out_ref[b : b + 1, 3 * rows :] = score_rows(turned, tail, far_ref)


def softmax(scores):
    peak = jnp.max(scores, axis=0, keepdims=True)
    unnorm = jnp.exp(scores - peak)
    return unnorm / jnp.sum(unnorm, axis=0, keepdims=True)


def band_pairs(parts):
    return [[(a + d) % parts for d in range(parts // 2 + (parts % 2 or a < parts // 2))] for a in range(parts)]


def moment(weights, component, rows_ref, columns_ref, layout, extra=None):
    picked = lax.broadcasted_iota(jnp.int32, weights.shape, 0) == component
    row = jnp.sum(jnp.where(picked, weights, 0.0), axis=0, keepdims=True)
    blocks, products = {}, {}
    for a, bands in enumerate(band_pairs(layout.parts)):
        left = list(split_two(columns_ref[a * LANES : (a + 1) * LANES, :] * row))
        adds = extra is not None and any(b not in products for b in bands)
        if adds:
            left.append(extra)
        both = jnp.dot(
            jnp.concatenate(left, axis=0),
            rows_ref[:, a * LANES : (a + len(bands)) * LANES],
            preferred_element_type=jnp.float32,
        )
        for d, b in enumerate(bands):
            part = both[:, d * LANES : (d + 1) * LANES]
            blocks[a, b] = part[:LANES] + part[LANES : 2 * LANES]
            if adds:
                products[b] = part[2 * LANES :]
    return blocks, products


def pair_masks():
    i = lax.broadcasted_iota(jnp.int32, (LANES, LANES), 0)
    j = lax.broadcasted_iota(jnp.int32, (LANES, LANES), 1)
    return i, j


class Layout:
    def __init__(self, width, comps):
        self.parts = width // LANES
        self.comps = comps
        self.pairs = [(a, b) for a, bands in enumerate(band_pairs(self.parts)) for b in bands[1:]]
        off = self.parts * (self.parts - 1) // 2 * LANES
        folded = self.parts // 2 * LANES + self.parts % 2 * (LANES // 2)
        self.diagonals = off + folded
        self.firsts = self.diagonals + -(-self.parts // 8) * 8
        self.counts = self.firsts + self.parts * comps
        self.half = -(-(self.counts + comps) // 16) * 8
        self.rows = self.half + HEAD

    def write(self, out_ref, flip, at, value):
        done = 0
        while done < value.shape[0]:
            side, row = divmod(at + done, self.half)
            count = min(value.shape[0] - done, self.half - row)
            out_ref[side ^ flip, row : row + count, :] = value[done : done + count]
            done += count


def store_second(blocks, normalizer, layout, out_ref, flip):
    parts = layout.parts
    largest = jnp.zeros((1, 1), jnp.float32)
    for a in range(parts):
        largest = jnp.maximum(largest, jnp.max(jnp.abs(blocks[a, a]), keepdims=True))
    exponent = exponent_of(largest * normalizer)
    factor = normalizer * power(-exponent)
    i, j = pair_masks()
    at = 0
    for a, b in layout.pairs:
        layout.write(out_ref, flip, at, blocks[a, b] * factor)
        at += LANES
    diagonal = [blocks[a, a] * factor for a in range(parts)]
    for a in range(0, parts - 1, 2):
        layout.write(out_ref, flip, at, jnp.where(i <= j, diagonal[a], diagonal[a + 1]))
        at += LANES
    if parts % 2:
        half = LANES // 2
        lower = pltpu.roll(diagonal[-1][half:], half, 1)
        layout.write(out_ref, flip, at, jnp.where(i <= j, diagonal[-1], 0.0)[:half] + jnp.where((i > j)[:half], lower, 0.0))
        at += half
    lines = [jnp.sum(jnp.where(i == j, d, 0.0), axis=0, keepdims=True) for d in diagonal]
    lines += [jnp.zeros((1, LANES), jnp.float32)] * (layout.firsts - at - parts)
    layout.write(out_ref, flip, at, jnp.concatenate(lines, axis=0))
    for side in range(2):
        out_ref[side, layout.half : layout.half + 1, :] = jnp.broadcast_to(exponent, (1, LANES))


def part_ways(table_ref, flip, outs):
    outs[0][...] = table_ref[flip]
    outs[1][...] = table_ref[1 - flip]


def store_low(low_ref, layout, out_ref, flip):
    body = low_ref.shape[0] - HEAD
    layout.write(out_ref, flip, layout.firsts, low_ref[:body, :])
    for side in range(2):
        out_ref[side, layout.half + 1 :, :] = low_ref[body + 1 :, :]


def own_place(me):
    return ((me >> 1) & 1) | ((me & 1) << 1)


def span(place, rows):
    return pl.ds(pl.multiple_of(place * rows, LANES), rows)


def place_here():
    return lax.axis_index("blk"), lax.axis_index("rows") & 1


def turn_kernel(*refs):
    blocks, (rows_ref, columns_ref) = refs[:-2], refs[-2:]
    rows, width = blocks[0].shape
    own = own_place(place_here()[0])
    for part, block_ref in enumerate(blocks):
        block = block_ref[...]
        rows_ref[span(part ^ own, rows), :width] = block
        rows_ref[span(part ^ own, rows), width:] = block[:, : rows_ref.shape[1] - width]
        columns_ref[:, span(part ^ own, rows)] = block.T.astype(jnp.float32)


def give_kernel(offsets, normalizer, layout, *refs):
    scores, (rows_ref, columns_ref), refs = refs[:4], refs[4:6], refs[6:]
    resp_ref, low_ref, here_ref, *outs, table_ref, message_ref = refs
    comps, rows = here_ref.shape
    me, flip = place_here()
    own = own_place(me)
    for source, score_ref in enumerate(scores):
        for b in range(score_ref.shape[0]):
            for part in range(4):
                to = part ^ (((source & 1) << 1) | (source >> 1)) ^ own
                table_ref[pl.ds(me ^ (4 * b + source), 1), span(to, rows)] = score_ref[
                    b : b + 1, part * rows : (part + 1) * rows
                ]
    weights = softmax(table_ref[...])
    resp_ref[...] = weights
    here_ref[...] = resp_ref[:, span(own, rows)]
    high = weights.astype(jnp.bfloat16).astype(jnp.float32)
    rest = weights - high
    middle = rest.astype(jnp.bfloat16).astype(jnp.float32)
    pieces = [high, middle, rest - middle]
    if 3 * comps % 16:
        pieces.append(jnp.zeros((-3 * comps % 16, 4 * rows), jnp.float32))
    stacked = jnp.concatenate(pieces, axis=0).astype(jnp.bfloat16)
    totals, products = [], {}
    for offset in offsets:
        total, product = moment(weights, me ^ offset, rows_ref, columns_ref, layout, None if products else stacked)
        totals.append(total)
        products = products or product
    product = jnp.concatenate([products[b] for b in range(layout.parts)], axis=1)
    first = (product[:comps] + (product[comps : 2 * comps] + product[2 * comps : 3 * comps])) * normalizer
    count = jnp.sum(weights, axis=1, keepdims=True) * normalizer
    exponent = exponent_of(jnp.max(jnp.abs(first), keepdims=True))
    first = first * power(-exponent)
    body = low_ref.shape[0] - HEAD
    low_ref[...] = jnp.zeros_like(low_ref)
    for a in range(layout.parts):
        low_ref[a * comps : (a + 1) * comps, :] = first[:, a * LANES : (a + 1) * LANES]
    at = layout.parts * comps
    low_ref[at : at + comps, :] = jnp.broadcast_to(count, (comps, LANES))
    low_ref[body:, :] = jnp.broadcast_to(exponent, (HEAD, LANES))
    for at, total in enumerate(totals):
        store_second(total, normalizer, layout, message_ref, 0)
        store_low(low_ref, layout, message_ref, 0)
        part_ways(message_ref, flip, outs[2 * at : 2 * at + 2])


def keep_kernel(normalizer, layout, resp_ref, low_ref, rows_ref, columns_ref, *refs):
    outs, message_ref = refs[:2], refs[2]
    me, flip = place_here()
    store_second(moment(resp_ref[...], me, rows_ref, columns_ref, layout)[0], normalizer, layout, message_ref, 0)
    store_low(low_ref, layout, message_ref, 0)
    part_ways(message_ref, flip, outs)


def tree(values):
    while len(values) > 1:
        values = [values[i] + values[i + 1] for i in range(0, len(values), 2)]
    return values[0]


def decoded_sum(refs, side, layout):
    row = lax.broadcasted_iota(jnp.int32, (layout.half, LANES), 0) + side * layout.half
    is_second, is_first = row < layout.firsts, row < layout.counts

    def at_rows(second, first):
        return jnp.where(is_second, power(second), jnp.where(is_first, power(first), 1.0))

    seconds = [r[layout.half : layout.half + 1, :] for r in refs]
    firsts = [r[layout.half + 1 : layout.half + 2, :] for r in refs]
    total = tree([r[: layout.half, :] * at_rows(s, f) for r, s, f in zip(refs, seconds, firsts, strict=True)])
    return total, seconds, firsts, at_rows


def highest(values):
    return values[0] if len(values) == 1 else jnp.maximum(values[0], highest(values[1:]))


def combine_kernel(layout, *refs):
    refs, out_ref = refs[:-1], refs[-1]
    total, seconds, firsts, at_rows = decoded_sum(refs, place_here()[1], layout)
    grow = float((len(refs) - 1).bit_length())
    second, first = highest(seconds) + grow, highest(firsts) + grow
    out_ref[: layout.half, :] = total * at_rows(-second, -first)
    out_ref[layout.half :, :] = jnp.broadcast_to(first, (HEAD, LANES))
    out_ref[layout.half : layout.half + 1, :] = second


def finish_kernel(layout, count, *refs):
    mine, others = refs[:count], refs[count : 2 * count]
    second_ref, first_ref, count_ref, table_ref = refs[2 * count :]
    side = place_here()[1]
    for part, messages in ((0, mine), (1, others)):
        total, _, _, _ = decoded_sum(messages, side ^ part, layout)
        table_ref[pl.ds(pl.multiple_of((side ^ part) * layout.half, 8), layout.half), :] = total
    parts, comps = layout.parts, layout.comps
    i, j = pair_masks()

    def place(a, b, block):
        second_ref[a * LANES : (a + 1) * LANES, b * LANES : (b + 1) * LANES] = block

    at = 0
    for a, b in layout.pairs:
        block = table_ref[at : at + LANES, :]
        place(a, b, block)
        place(b, a, block.T)
        at += LANES
    lines = [table_ref[layout.diagonals + a : layout.diagonals + a + 1, :] for a in range(parts)]
    for a in range(0, parts - 1, 2):
        block = table_ref[at : at + LANES, :]
        turned = block.T
        place(a, a, jnp.where(i <= j, block, turned))
        place(a + 1, a + 1, jnp.where(i == j, lines[a + 1], jnp.where(i > j, block, turned)))
        at += LANES
    if parts % 2:
        half = LANES // 2
        block = table_ref[at : at + half, :]
        upper = jnp.where((i <= j)[:half], block, 0.0)
        lower = pltpu.roll(jnp.where((i > j)[:half], block, 0.0), half, 1)
        whole = jnp.concatenate([upper, lower], axis=0)
        place(parts - 1, parts - 1, jnp.where(i == j, lines[-1], whole + whole.T))
    at = layout.firsts
    for a in range(parts):
        first_ref[:, a * LANES : (a + 1) * LANES] = table_ref[at : at + comps, :]
        at += comps
    count_ref[...] = table_ref[at : at + comps, :].T[0:1, :]


def call(kernel, out_shape, args, flops, scratch=()):
    specs = [pl.BlockSpec(memory_space=pltpu.VMEM)] * len(args)
    moved = sum(a.size * a.dtype.itemsize for a in args) + sum(
        o.size * o.dtype.itemsize for o in jax.tree.leaves(out_shape)
    )
    return pl.pallas_call(
        kernel,
        out_shape=out_shape,
        in_specs=specs,
        out_specs=jax.tree.map(lambda _: pl.BlockSpec(memory_space=pltpu.VMEM), out_shape),
        scratch_shapes=list(scratch),
        compiler_params=pltpu.CompilerParams(vmem_limit_bytes=VMEM_LIMIT),
        cost_estimate=pl.CostEstimate(flops=flops, bytes_accessed=moved, transcendentals=0),
    )(*args)


def solution(mesh):
    n_blk, n_rows = mesh.shape["blk"], mesh.shape["rows"]
    groups = n_blk // 4

    def hop(value, blk, rows):
        if rows == 0:
            return lax.ppermute(value, "blk", [(i, i ^ blk) for i in range(n_blk)])
        if blk == 0:
            return lax.ppermute(value, "rows", [(i, i ^ rows) for i in range(n_rows)])
        pairs = [
            (i * n_rows + j, (i ^ blk) * n_rows + (j ^ rows)) for i in range(n_blk) for j in range(n_rows)
        ]
        return lax.ppermute(value, ("blk", "rows"), pairs)

    def shards(embeddings, factors, centres, log_prior):
        rows, width = embeddings.shape
        comps = factors.shape[0] * n_blk
        normalizer = comps / (rows * n_blk * n_rows)
        layout = Layout(width, comps)
        low_rows = 2 * layout.half - layout.firsts + HEAD

        near = hop(embeddings, 2, 0)
        matrix = factors.reshape(width, width)
        tail = jnp.concatenate(
            [
                centres,
                jnp.broadcast_to(log_prior[:, None], (1, width)),
                jnp.zeros((TAIL - 2, width), jnp.bfloat16),
            ],
            axis=0,
        )
        core = hop(embeddings, 1, 0)
        matrices = [hop(matrix, 4 * b, 0) for b in range(1, groups)]
        tails = [hop(tail, 4 * b, 0) for b in range(1, groups)]
        flops = 2 * rows * width * width
        line = lambda count, lanes: jax.ShapeDtypeStruct((count, lanes * rows), jnp.float32)
        turned = jax.ShapeDtypeStruct((width, width), jnp.bfloat16)
        own_scores, own_turned = call(
            own_kernel, (line(1, 2), turned), (embeddings, core, matrix, tail), 2 * flops
        )
        near, matrices, tails, own_scores = lax.optimization_barrier((near, matrices, tails, own_scores))
        far = hop(near, 1, 0)
        tails = [tail] + tails
        most_scores, other_turned = call(
            lambda *refs: near_kernel(groups, *refs),
            (line(groups, 3), jax.ShapeDtypeStruct((groups - 1, width, width), jnp.bfloat16)),
            (embeddings, near, core, own_scores, own_turned, *tails, *matrices),
            (3 * groups - 2) * flops,
        )
        scores = call(
            lambda *refs: far_kernel(groups, *refs),
            line(groups, 4),
            (far, most_scores, own_turned, other_turned, *tails),
            groups * flops,
        )
        scores, far = lax.optimization_barrier((scores, far))
        blocks = (embeddings, near, core, far)
        both = call(
            turn_kernel,
            (
                jax.ShapeDtypeStruct((4 * rows, width + layout.parts // 2 * LANES), jnp.bfloat16),
                jax.ShapeDtypeStruct((width, 4 * rows), jnp.float32),
            ),
            blocks,
            0,
        )
        near_scores = hop(scores, 2, 0)
        core_scores = hop(scores, 1, 0)
        far_scores = hop(near_scores, 1, 0)

        sent = jax.ShapeDtypeStruct((layout.rows, LANES), jnp.float32)
        whole = pltpu.VMEM((2, layout.rows, LANES), jnp.float32)
        flops = 4 * 4 * rows * width * width
        resp, low, here, *given = call(
            lambda *refs: give_kernel([4 * b for b in range(1, groups)], normalizer, layout, *refs),
            (
                jax.ShapeDtypeStruct((comps, 4 * rows), jnp.float32),
                jax.ShapeDtypeStruct((low_rows, LANES), jnp.float32),
                jax.ShapeDtypeStruct((comps, rows), jnp.float32),
                *[sent] * (2 * groups - 2),
            ),
            (scores, core_scores, near_scores, far_scores, *both),
            flops * (groups - 1),
            [pltpu.VMEM((comps, 4 * rows), jnp.float32), whole],
        )
        received = {}
        for b in range(1, groups):
            for z in (1, 0):
                received[b, z] = hop(given[2 * b - 2 + z].astype(jnp.float16), 4 * b, z)
        kept = call(
            lambda *refs: keep_kernel(normalizer, layout, *refs),
            (sent, sent),
            (resp, low, *both),
            flops,
            [whole],
        )
        received[0, 0] = lax.optimization_barrier(kept[0].astype(jnp.float16))
        received[0, 1] = hop(kept[1].astype(jnp.float16), 0, 1)
        for b in range(1, groups):
            received[b, 0], received[b, 1] = lax.optimization_barrier((received[b, 0], received[b, 1]))
        wide = {key: value.astype(jnp.float32) for key, value in received.items()}
        same = [wide[b, 0] for b in range(groups)]
        other = [wide[b, 1] for b in range(1, groups)]
        summed = call(
            lambda *refs: combine_kernel(layout, *refs), sent, (*same, wide[0, 1], *other), 0
        )
        summed = lax.optimization_barrier(summed.astype(jnp.float16))
        bit = 2
        while 2 * bit < n_rows:
            messages = [m.astype(jnp.float32) for m in (summed, hop(summed, 0, bit))]
            summed = call(
                lambda *refs: combine_kernel(layout, *refs), sent, messages, 0
            )
            summed = lax.optimization_barrier(summed.astype(jnp.float16))
            bit *= 2
        last = [0, bit] if bit < n_rows else [0]
        others = [hop(summed, 0, 1 ^ z) for z in reversed(last)][::-1]
        mine = [summed] + [hop(summed, 0, z) for z in last[1:]]
        second, first, count = call(
            lambda *refs: finish_kernel(layout, len(last), *refs),
            (
                jax.ShapeDtypeStruct((width, width), jnp.float32),
                jax.ShapeDtypeStruct((comps, width), jnp.float32),
                jax.ShapeDtypeStruct((1, comps), jnp.float32),
            ),
            [m.astype(jnp.float32) for m in mine + others],
            0,
            [pltpu.VMEM((2 * layout.half, LANES), jnp.float32)],
        )
        return here, count.reshape(comps), first, second.reshape(1, width, width)

    in_specs = (P(("blk", "rows"), None), P("blk", None, None), P("blk", None), P("blk"))
    out_specs = (P(None, ("blk", "rows")), P(), P(), P("blk", None, None))
    return jax.shard_map(shards, mesh=mesh, in_specs=in_specs, out_specs=out_specs, check_vma=False)
```

```python
import jax
import jax.numpy as jnp
from jax import lax
from jax.experimental import pallas as pl
from jax.experimental.pallas import tpu as pltpu
from jax.sharding import PartitionSpec as P

half_temper = 0.05
LANES = 128
TAIL = 16
HEAD = 8
VMEM_LIMIT = 40 * 1024 * 1024
NT = (((1,), (1,)), ((), ()))


def split_two(value):
    high = value.astype(jnp.bfloat16)
    low = (value - high.astype(jnp.float32)).astype(jnp.bfloat16)
    return high, low


def power(exponent):
    whole = exponent.astype(jnp.int32)
    size = jnp.abs(whole)
    result = jnp.ones(exponent.shape, jnp.float32)
    for bit in range(7):
        factor = jnp.where(whole < 0, 0.5 ** (1 << bit), 2.0 ** (1 << bit))
        result = result * jnp.where((size >> bit) & 1 == 1, factor, 1.0)
    return result


def exponent_of(largest):
    bits = jnp.ceil(jnp.log(jnp.maximum(largest, 1e-35)) * 1.4426950408889634) - 12.0
    return jnp.clip(bits, -110.0, 110.0)


def score_rows(turned, tail, rows_ref):
    whitened = lax.dot_general(turned, rows_ref[...], NT, preferred_element_type=jnp.float32)
    whitened = whitened - tail.T[:, 0:1]
    return tail[1:2, 0:1] - half_temper * jnp.sum(whitened * whitened, axis=0, keepdims=True)


def own_kernel(own_ref, core_ref, matrix_ref, tail_ref, out_ref, turned_ref):
    rows = own_ref.shape[0]
    turned_ref[...] = matrix_ref[...].T
    tail = tail_ref[...].astype(jnp.float32)
    for part, rows_ref in enumerate((own_ref, core_ref)):
        out_ref[:, part * rows : (part + 1) * rows] = score_rows(turned_ref[...], tail, rows_ref)


def near_kernel(groups, own_ref, near_ref, core_ref, done_ref, turned_ref, *refs):
    tails, matrices, (out_ref, others_ref) = refs[:groups], refs[groups : 2 * groups - 1], refs[2 * groups - 1 :]
    rows = own_ref.shape[0]
    for b in range(groups):
        if b:
            others_ref[b - 1] = matrices[b - 1][...].T
        turned = others_ref[b - 1] if b else turned_ref[...]
        tail = tails[b][...].astype(jnp.float32)
        for part, rows_ref in enumerate((own_ref, near_ref, core_ref)):
            if b == 0 and part != 1:
                line = done_ref[:, part // 2 * rows : (part // 2 + 1) * rows]
            else:
                line = score_rows(turned, tail, rows_ref)
            out_ref[b : b + 1, part * rows : (part + 1) * rows] = line


def far_kernel(groups, far_ref, done_ref, turned_ref, others_ref, *refs):
    tails, out_ref = refs[:groups], refs[groups]
    rows = far_ref.shape[0]
    out_ref[:, : 3 * rows] = done_ref[...]
    for b in range(groups):
        tail = tails[b][...].astype(jnp.float32)
        turned = others_ref[b - 1] if b else turned_ref[...]
        out_ref[b : b + 1, 3 * rows :] = score_rows(turned, tail, far_ref)


def softmax(scores):
    peak = jnp.max(scores, axis=0, keepdims=True)
    unnorm = jnp.exp(scores - peak)
    return unnorm / jnp.sum(unnorm, axis=0, keepdims=True)


def band_pairs(parts):
    return [[(a + d) % parts for d in range(parts // 2 + (parts % 2 or a < parts // 2))] for a in range(parts)]


def moment(weights, component, rows_ref, columns_ref, layout, extra=None):
    picked = lax.broadcasted_iota(jnp.int32, weights.shape, 0) == component
    row = jnp.sum(jnp.where(picked, weights, 0.0), axis=0, keepdims=True)
    blocks, products = {}, {}
    for a, bands in enumerate(band_pairs(layout.parts)):
        left = list(split_two(columns_ref[a * LANES : (a + 1) * LANES, :] * row))
        adds = extra is not None and any(b not in products for b in bands)
        if adds:
            left.append(extra)
        both = jnp.dot(
            jnp.concatenate(left, axis=0),
            rows_ref[:, a * LANES : (a + len(bands)) * LANES],
            preferred_element_type=jnp.float32,
        )
        for d, b in enumerate(bands):
            part = both[:, d * LANES : (d + 1) * LANES]
            blocks[a, b] = part[:LANES] + part[LANES : 2 * LANES]
            if adds:
                products[b] = part[2 * LANES :]
    return blocks, products


def pair_masks():
    i = lax.broadcasted_iota(jnp.int32, (LANES, LANES), 0)
    j = lax.broadcasted_iota(jnp.int32, (LANES, LANES), 1)
    return i, j


class Layout:
    def __init__(self, width, comps):
        self.parts = width // LANES
        self.comps = comps
        self.pairs = [(a, b) for a, bands in enumerate(band_pairs(self.parts)) for b in bands[1:]]
        off = self.parts * (self.parts - 1) // 2 * LANES
        folded = self.parts // 2 * LANES + self.parts % 2 * (LANES // 2)
        self.diagonals = off + folded
        self.firsts = self.diagonals + -(-self.parts // 8) * 8
        self.counts = self.firsts + self.parts * comps
        self.half = -(-(self.counts + comps) // 16) * 8
        self.rows = self.half + HEAD

    def write(self, out_ref, flip, at, value):
        done = 0
        while done < value.shape[0]:
            side, row = divmod(at + done, self.half)
            count = min(value.shape[0] - done, self.half - row)
            out_ref[side ^ flip, row : row + count, :] = value[done : done + count]
            done += count


def store_second(blocks, normalizer, layout, out_ref, flip):
    parts = layout.parts
    largest = jnp.zeros((1, 1), jnp.float32)
    for a in range(parts):
        largest = jnp.maximum(largest, jnp.max(jnp.abs(blocks[a, a]), keepdims=True))
    exponent = exponent_of(largest * normalizer)
    factor = normalizer * power(-exponent)
    i, j = pair_masks()
    at = 0
    for a, b in layout.pairs:
        layout.write(out_ref, flip, at, blocks[a, b] * factor)
        at += LANES
    diagonal = [blocks[a, a] * factor for a in range(parts)]
    for a in range(0, parts - 1, 2):
        layout.write(out_ref, flip, at, jnp.where(i <= j, diagonal[a], diagonal[a + 1]))
        at += LANES
    if parts % 2:
        half = LANES // 2
        lower = pltpu.roll(diagonal[-1][half:], half, 1)
        layout.write(out_ref, flip, at, jnp.where(i <= j, diagonal[-1], 0.0)[:half] + jnp.where((i > j)[:half], lower, 0.0))
        at += half
    lines = [jnp.sum(jnp.where(i == j, d, 0.0), axis=0, keepdims=True) for d in diagonal]
    lines += [jnp.zeros((1, LANES), jnp.float32)] * (layout.firsts - at - parts)
    layout.write(out_ref, flip, at, jnp.concatenate(lines, axis=0))
    for side in range(2):
        out_ref[side, layout.half : layout.half + 1, :] = jnp.broadcast_to(exponent, (1, LANES))


def part_ways(table_ref, flip, outs):
    outs[0][...] = table_ref[flip]
    outs[1][...] = table_ref[1 - flip]


def store_low(low_ref, layout, out_ref, flip):
    body = low_ref.shape[0] - HEAD
    layout.write(out_ref, flip, layout.firsts, low_ref[:body, :])
    for side in range(2):
        out_ref[side, layout.half + 1 :, :] = low_ref[body + 1 :, :]


def own_place(me):
    return ((me >> 1) & 1) | ((me & 1) << 1)


def span(place, rows):
    return pl.ds(pl.multiple_of(place * rows, LANES), rows)


def place_here():
    return lax.axis_index("blk"), lax.axis_index("rows") & 1


def turn_kernel(*refs):
    blocks, (rows_ref, columns_ref) = refs[:-2], refs[-2:]
    rows, width = blocks[0].shape
    own = own_place(place_here()[0])
    for part, block_ref in enumerate(blocks):
        block = block_ref[...]
        rows_ref[span(part ^ own, rows), :width] = block
        rows_ref[span(part ^ own, rows), width:] = block[:, : rows_ref.shape[1] - width]
        columns_ref[:, span(part ^ own, rows)] = block.T.astype(jnp.float32)


def give_kernel(offsets, normalizer, layout, *refs):
    scores, (rows_ref, columns_ref), refs = refs[:4], refs[4:6], refs[6:]
    resp_ref, low_ref, here_ref, *outs, message_ref = refs
    comps, rows = here_ref.shape
    me, flip = place_here()
    own = own_place(me)
    index = lax.broadcasted_iota(jnp.int32, (comps, 4 * rows), 0)
    table = jnp.zeros((comps, 4 * rows), jnp.float32)
    for source, score_ref in enumerate(scores):
        turn = ((source & 1) << 1) | (source >> 1)
        for b in range(score_ref.shape[0]):
            pieces = [score_ref[b : b + 1, (part ^ turn) * rows : ((part ^ turn) + 1) * rows] for part in range(4)]
            table = jnp.where(index == (me ^ (4 * b + source)), jnp.concatenate(pieces, axis=1), table)
    weights = softmax(table)
    here_ref[...] = weights[:, :rows]
    for part in range(4):
        resp_ref[:, span(part ^ own, rows)] = weights[:, part * rows : (part + 1) * rows]
    weights = resp_ref[...]
    high = weights.astype(jnp.bfloat16).astype(jnp.float32)
    rest = weights - high
    middle = rest.astype(jnp.bfloat16).astype(jnp.float32)
    pieces = [high, middle, rest - middle]
    if 3 * comps % 16:
        pieces.append(jnp.zeros((-3 * comps % 16, 4 * rows), jnp.float32))
    stacked = jnp.concatenate(pieces, axis=0).astype(jnp.bfloat16)
    totals, products = [], {}
    for offset in offsets:
        total, product = moment(weights, me ^ offset, rows_ref, columns_ref, layout, None if products else stacked)
        totals.append(total)
        products = products or product
    product = jnp.concatenate([products[b] for b in range(layout.parts)], axis=1)
    first = (product[:comps] + (product[comps : 2 * comps] + product[2 * comps : 3 * comps])) * normalizer
    count = jnp.sum(weights, axis=1, keepdims=True) * normalizer
    exponent = exponent_of(jnp.max(jnp.abs(first), keepdims=True))
    first = first * power(-exponent)
    body = low_ref.shape[0] - HEAD
    low_ref[...] = jnp.zeros_like(low_ref)
    for a in range(layout.parts):
        low_ref[a * comps : (a + 1) * comps, :] = first[:, a * LANES : (a + 1) * LANES]
    at = layout.parts * comps
    low_ref[at : at + comps, :] = jnp.broadcast_to(count, (comps, LANES))
    low_ref[body:, :] = jnp.broadcast_to(exponent, (HEAD, LANES))
    for at, total in enumerate(totals):
        store_second(total, normalizer, layout, message_ref, 0)
        store_low(low_ref, layout, message_ref, 0)
        part_ways(message_ref, flip, outs[2 * at : 2 * at + 2])


def keep_kernel(normalizer, layout, resp_ref, low_ref, rows_ref, columns_ref, *refs):
    outs, message_ref = refs[:2], refs[2]
    me, flip = place_here()
    store_second(moment(resp_ref[...], me, rows_ref, columns_ref, layout)[0], normalizer, layout, message_ref, 0)
    store_low(low_ref, layout, message_ref, 0)
    part_ways(message_ref, flip, outs)


def tree(values):
    while len(values) > 1:
        values = [values[i] + values[i + 1] for i in range(0, len(values), 2)]
    return values[0]


def decoded_sum(refs, side, layout):
    row = lax.broadcasted_iota(jnp.int32, (layout.half, LANES), 0) + side * layout.half
    is_second, is_first = row < layout.firsts, row < layout.counts

    def at_rows(second, first):
        return jnp.where(is_second, power(second), jnp.where(is_first, power(first), 1.0))

    seconds = [r[layout.half : layout.half + 1, :] for r in refs]
    firsts = [r[layout.half + 1 : layout.half + 2, :] for r in refs]
    total = tree([r[: layout.half, :] * at_rows(s, f) for r, s, f in zip(refs, seconds, firsts, strict=True)])
    return total, seconds, firsts, at_rows


def highest(values):
    return values[0] if len(values) == 1 else jnp.maximum(values[0], highest(values[1:]))


def combine_kernel(layout, *refs):
    refs, out_ref = refs[:-1], refs[-1]
    total, seconds, firsts, at_rows = decoded_sum(refs, place_here()[1], layout)
    grow = float((len(refs) - 1).bit_length())
    second, first = highest(seconds) + grow, highest(firsts) + grow
    out_ref[: layout.half, :] = total * at_rows(-second, -first)
    out_ref[layout.half :, :] = jnp.broadcast_to(first, (HEAD, LANES))
    out_ref[layout.half : layout.half + 1, :] = second


def finish_kernel(layout, count, *refs):
    mine, others = refs[:count], refs[count : 2 * count]
    second_ref, first_ref, count_ref, table_ref = refs[2 * count :]
    side = place_here()[1]
    for part, messages in ((0, mine), (1, others)):
        total, _, _, _ = decoded_sum(messages, side ^ part, layout)
        table_ref[pl.ds(pl.multiple_of((side ^ part) * layout.half, 8), layout.half), :] = total
    parts, comps = layout.parts, layout.comps
    i, j = pair_masks()

    def place(a, b, block):
        second_ref[a * LANES : (a + 1) * LANES, b * LANES : (b + 1) * LANES] = block

    at = 0
    for a, b in layout.pairs:
        block = table_ref[at : at + LANES, :]
        place(a, b, block)
        place(b, a, block.T)
        at += LANES
    lines = [table_ref[layout.diagonals + a : layout.diagonals + a + 1, :] for a in range(parts)]
    for a in range(0, parts - 1, 2):
        block = table_ref[at : at + LANES, :]
        turned = block.T
        place(a, a, jnp.where(i <= j, block, turned))
        place(a + 1, a + 1, jnp.where(i == j, lines[a + 1], jnp.where(i > j, block, turned)))
        at += LANES
    if parts % 2:
        half = LANES // 2
        block = table_ref[at : at + half, :]
        upper = jnp.where((i <= j)[:half], block, 0.0)
        lower = pltpu.roll(jnp.where((i > j)[:half], block, 0.0), half, 1)
        whole = jnp.concatenate([upper, lower], axis=0)
        place(parts - 1, parts - 1, jnp.where(i == j, lines[-1], whole + whole.T))
    at = layout.firsts
    for a in range(parts):
        first_ref[:, a * LANES : (a + 1) * LANES] = table_ref[at : at + comps, :]
        at += comps
    count_ref[...] = table_ref[at : at + comps, :].T[0:1, :]


def call(kernel, out_shape, args, flops, scratch=()):
    specs = [pl.BlockSpec(memory_space=pltpu.VMEM)] * len(args)
    moved = sum(a.size * a.dtype.itemsize for a in args) + sum(
        o.size * o.dtype.itemsize for o in jax.tree.leaves(out_shape)
    )
    return pl.pallas_call(
        kernel,
        out_shape=out_shape,
        in_specs=specs,
        out_specs=jax.tree.map(lambda _: pl.BlockSpec(memory_space=pltpu.VMEM), out_shape),
        scratch_shapes=list(scratch),
        compiler_params=pltpu.CompilerParams(vmem_limit_bytes=VMEM_LIMIT),
        cost_estimate=pl.CostEstimate(flops=flops, bytes_accessed=moved, transcendentals=0),
    )(*args)


def solution(mesh):
    n_blk, n_rows = mesh.shape["blk"], mesh.shape["rows"]
    groups = n_blk // 4

    def hop(value, blk, rows):
        if rows == 0:
            return lax.ppermute(value, "blk", [(i, i ^ blk) for i in range(n_blk)])
        if blk == 0:
            return lax.ppermute(value, "rows", [(i, i ^ rows) for i in range(n_rows)])
        pairs = [
            (i * n_rows + j, (i ^ blk) * n_rows + (j ^ rows)) for i in range(n_blk) for j in range(n_rows)
        ]
        return lax.ppermute(value, ("blk", "rows"), pairs)

    def shards(embeddings, factors, centres, log_prior):
        rows, width = embeddings.shape
        comps = factors.shape[0] * n_blk
        normalizer = comps / (rows * n_blk * n_rows)
        layout = Layout(width, comps)
        low_rows = 2 * layout.half - layout.firsts + HEAD

        near = hop(embeddings, 2, 0)
        matrix = factors.reshape(width, width)
        tail = jnp.concatenate(
            [
                centres,
                jnp.broadcast_to(log_prior[:, None], (1, width)),
                jnp.zeros((TAIL - 2, width), jnp.bfloat16),
            ],
            axis=0,
        )
        core = hop(embeddings, 1, 0)
        matrices = [hop(matrix, 4 * b, 0) for b in range(1, groups)]
        tails = [hop(tail, 4 * b, 0) for b in range(1, groups)]
        flops = 2 * rows * width * width
        line = lambda count, lanes: jax.ShapeDtypeStruct((count, lanes * rows), jnp.float32)
        turned = jax.ShapeDtypeStruct((width, width), jnp.bfloat16)
        own_scores, own_turned = call(
            own_kernel, (line(1, 2), turned), (embeddings, core, matrix, tail), 2 * flops
        )
        near, matrices, tails, own_scores = lax.optimization_barrier((near, matrices, tails, own_scores))
        far = hop(near, 1, 0)
        tails = [tail] + tails
        most_scores, other_turned = call(
            lambda *refs: near_kernel(groups, *refs),
            (line(groups, 3), jax.ShapeDtypeStruct((groups - 1, width, width), jnp.bfloat16)),
            (embeddings, near, core, own_scores, own_turned, *tails, *matrices),
            (3 * groups - 2) * flops,
        )
        scores = call(
            lambda *refs: far_kernel(groups, *refs),
            line(groups, 4),
            (far, most_scores, own_turned, other_turned, *tails),
            groups * flops,
        )
        scores, far = lax.optimization_barrier((scores, far))
        blocks = (embeddings, near, core, far)
        both = call(
            turn_kernel,
            (
                jax.ShapeDtypeStruct((4 * rows, width + layout.parts // 2 * LANES), jnp.bfloat16),
                jax.ShapeDtypeStruct((width, 4 * rows), jnp.float32),
            ),
            blocks,
            0,
        )
        near_scores = hop(scores, 2, 0)
        core_scores = hop(scores, 1, 0)
        far_scores = hop(near_scores, 1, 0)

        sent = jax.ShapeDtypeStruct((layout.rows, LANES), jnp.float32)
        whole = pltpu.VMEM((2, layout.rows, LANES), jnp.float32)
        flops = 4 * 4 * rows * width * width
        resp, low, here, *given = call(
            lambda *refs: give_kernel([4 * b for b in range(1, groups)], normalizer, layout, *refs),
            (
                jax.ShapeDtypeStruct((comps, 4 * rows), jnp.float32),
                jax.ShapeDtypeStruct((low_rows, LANES), jnp.float32),
                jax.ShapeDtypeStruct((comps, rows), jnp.float32),
                *[sent] * (2 * groups - 2),
            ),
            (scores, core_scores, near_scores, far_scores, *both),
            flops * (groups - 1),
            [whole],
        )
        received = {}
        for b in range(1, groups):
            for z in (1, 0):
                received[b, z] = hop(given[2 * b - 2 + z].astype(jnp.float16), 4 * b, z)
        kept = call(
            lambda *refs: keep_kernel(normalizer, layout, *refs),
            (sent, sent),
            (resp, low, *both),
            flops,
            [whole],
        )
        received[0, 0] = lax.optimization_barrier(kept[0].astype(jnp.float16))
        received[0, 1] = hop(kept[1].astype(jnp.float16), 0, 1)
        for b in range(1, groups):
            received[b, 0], received[b, 1] = lax.optimization_barrier((received[b, 0], received[b, 1]))
        wide = {key: value.astype(jnp.float32) for key, value in received.items()}
        same = [wide[b, 0] for b in range(groups)]
        other = [wide[b, 1] for b in range(1, groups)]
        summed = call(
            lambda *refs: combine_kernel(layout, *refs), sent, (*same, wide[0, 1], *other), 0
        )
        summed = lax.optimization_barrier(summed.astype(jnp.float16))
        bit = 2
        while 2 * bit < n_rows:
            messages = [m.astype(jnp.float32) for m in (summed, hop(summed, 0, bit))]
            summed = call(
                lambda *refs: combine_kernel(layout, *refs), sent, messages, 0
            )
            summed = lax.optimization_barrier(summed.astype(jnp.float16))
            bit *= 2
        last = [0, bit] if bit < n_rows else [0]
        others = [hop(summed, 0, 1 ^ z) for z in reversed(last)][::-1]
        mine = [summed] + [hop(summed, 0, z) for z in last[1:]]
        second, first, count = call(
            lambda *refs: finish_kernel(layout, len(last), *refs),
            (
                jax.ShapeDtypeStruct((width, width), jnp.float32),
                jax.ShapeDtypeStruct((comps, width), jnp.float32),
                jax.ShapeDtypeStruct((1, comps), jnp.float32),
            ),
            [m.astype(jnp.float32) for m in mine + others],
            0,
            [pltpu.VMEM((2 * layout.half, LANES), jnp.float32)],
        )
        return here, count.reshape(comps), first, second.reshape(1, width, width)

    in_specs = (P(("blk", "rows"), None), P("blk", None, None), P("blk", None), P("blk"))
    out_specs = (P(None, ("blk", "rows")), P(), P(), P("blk", None, None))
    return jax.shard_map(shards, mesh=mesh, in_specs=in_specs, out_specs=out_specs, check_vma=False)
```

```python
import jax
import jax.numpy as jnp
from jax import lax
from jax.experimental import pallas as pl
from jax.experimental.pallas import tpu as pltpu
from jax.sharding import PartitionSpec as P

half_temper = 0.05
LANES = 128
TAIL = 16
HEAD = 8
VMEM_LIMIT = 40 * 1024 * 1024
NT = (((1,), (1,)), ((), ()))


def split_two(value):
    high = value.astype(jnp.bfloat16)
    low = (value - high.astype(jnp.float32)).astype(jnp.bfloat16)
    return high, low


def power(exponent):
    whole = exponent.astype(jnp.int32)
    size = jnp.abs(whole)
    result = jnp.ones(exponent.shape, jnp.float32)
    for bit in range(7):
        factor = jnp.where(whole < 0, 0.5 ** (1 << bit), 2.0 ** (1 << bit))
        result = result * jnp.where((size >> bit) & 1 == 1, factor, 1.0)
    return result


def exponent_of(largest):
    bits = jnp.ceil(jnp.log(jnp.maximum(largest, 1e-35)) * 1.4426950408889634) - 12.0
    return jnp.clip(bits, -110.0, 110.0)


def score_rows(turned, tail, rows_ref):
    whitened = lax.dot_general(turned, rows_ref[...], NT, preferred_element_type=jnp.float32)
    whitened = whitened - tail.T[:, 0:1]
    return tail[1:2, 0:1] - half_temper * jnp.sum(whitened * whitened, axis=0, keepdims=True)


def own_kernel(own_ref, matrix_ref, tail_ref, out_ref, turned_ref):
    turned_ref[...] = matrix_ref[...].T
    out_ref[...] = score_rows(turned_ref[...], tail_ref[...].astype(jnp.float32), own_ref)


def near_kernel(groups, own_ref, near_ref, core_ref, done_ref, turned_ref, *refs):
    tails, matrices, (out_ref, others_ref) = refs[:groups], refs[groups : 2 * groups - 1], refs[2 * groups - 1 :]
    rows = own_ref.shape[0]
    for b in range(groups):
        if b:
            others_ref[b - 1] = matrices[b - 1][...].T
        turned = others_ref[b - 1] if b else turned_ref[...]
        tail = tails[b][...].astype(jnp.float32)
        for part, rows_ref in enumerate((own_ref, near_ref, core_ref)):
            if b == 0 and part == 0:
                line = done_ref[...]
            else:
                line = score_rows(turned, tail, rows_ref)
            out_ref[b : b + 1, part * rows : (part + 1) * rows] = line


def far_kernel(groups, far_ref, done_ref, turned_ref, others_ref, *refs):
    tails, out_ref = refs[:groups], refs[groups]
    rows = far_ref.shape[0]
    out_ref[:, : 3 * rows] = done_ref[...]
    for b in range(groups):
        tail = tails[b][...].astype(jnp.float32)
        turned = others_ref[b - 1] if b else turned_ref[...]
        out_ref[b : b + 1, 3 * rows :] = score_rows(turned, tail, far_ref)


def softmax(scores):
    peak = jnp.max(scores, axis=0, keepdims=True)
    unnorm = jnp.exp(scores - peak)
    return unnorm / jnp.sum(unnorm, axis=0, keepdims=True)


def band_pairs(parts):
    return [[(a + d) % parts for d in range(parts // 2 + (parts % 2 or a < parts // 2))] for a in range(parts)]


def moment(weights, component, rows_ref, columns_ref, layout, extra=None):
    picked = lax.broadcasted_iota(jnp.int32, weights.shape, 0) == component
    row = jnp.sum(jnp.where(picked, weights, 0.0), axis=0, keepdims=True)
    blocks, products = {}, {}
    for a, bands in enumerate(band_pairs(layout.parts)):
        left = list(split_two(columns_ref[a * LANES : (a + 1) * LANES, :] * row))
        adds = extra is not None and any(b not in products for b in bands)
        if adds:
            left.append(extra)
        both = jnp.dot(
            jnp.concatenate(left, axis=0),
            rows_ref[:, a * LANES : (a + len(bands)) * LANES],
            preferred_element_type=jnp.float32,
        )
        for d, b in enumerate(bands):
            part = both[:, d * LANES : (d + 1) * LANES]
            blocks[a, b] = part[:LANES] + part[LANES : 2 * LANES]
            if adds:
                products[b] = part[2 * LANES :]
    return blocks, products


def pair_masks():
    i = lax.broadcasted_iota(jnp.int32, (LANES, LANES), 0)
    j = lax.broadcasted_iota(jnp.int32, (LANES, LANES), 1)
    return i, j


class Layout:
    def __init__(self, width, comps):
        self.parts = width // LANES
        self.comps = comps
        self.pairs = [(a, b) for a, bands in enumerate(band_pairs(self.parts)) for b in bands[1:]]
        off = self.parts * (self.parts - 1) // 2 * LANES
        folded = self.parts // 2 * LANES + self.parts % 2 * (LANES // 2)
        self.diagonals = off + folded
        self.firsts = self.diagonals + -(-self.parts // 8) * 8
        self.counts = self.firsts + self.parts * comps
        self.half = -(-(self.counts + comps) // 16) * 8
        self.rows = self.half + HEAD

    def write(self, out_ref, flip, at, value):
        done = 0
        while done < value.shape[0]:
            side, row = divmod(at + done, self.half)
            count = min(value.shape[0] - done, self.half - row)
            out_ref[side ^ flip, row : row + count, :] = value[done : done + count]
            done += count


def store_second(blocks, normalizer, layout, out_ref, flip):
    parts = layout.parts
    largest = jnp.zeros((1, 1), jnp.float32)
    for a in range(parts):
        largest = jnp.maximum(largest, jnp.max(jnp.abs(blocks[a, a]), keepdims=True))
    exponent = exponent_of(largest * normalizer)
    factor = normalizer * power(-exponent)
    i, j = pair_masks()
    at = 0
    for a, b in layout.pairs:
        layout.write(out_ref, flip, at, blocks[a, b] * factor)
        at += LANES
    diagonal = [blocks[a, a] * factor for a in range(parts)]
    for a in range(0, parts - 1, 2):
        layout.write(out_ref, flip, at, jnp.where(i <= j, diagonal[a], diagonal[a + 1]))
        at += LANES
    if parts % 2:
        half = LANES // 2
        lower = pltpu.roll(diagonal[-1][half:], half, 1)
        layout.write(out_ref, flip, at, jnp.where(i <= j, diagonal[-1], 0.0)[:half] + jnp.where((i > j)[:half], lower, 0.0))
        at += half
    lines = [jnp.sum(jnp.where(i == j, d, 0.0), axis=0, keepdims=True) for d in diagonal]
    lines += [jnp.zeros((1, LANES), jnp.float32)] * (layout.firsts - at - parts)
    layout.write(out_ref, flip, at, jnp.concatenate(lines, axis=0))
    for side in range(2):
        out_ref[side, layout.half : layout.half + 1, :] = jnp.broadcast_to(exponent, (1, LANES))


def part_ways(table_ref, flip, outs):
    outs[0][...] = table_ref[flip]
    outs[1][...] = table_ref[1 - flip]


def store_low(low_ref, layout, out_ref, flip):
    body = low_ref.shape[0] - HEAD
    layout.write(out_ref, flip, layout.firsts, low_ref[:body, :])
    for side in range(2):
        out_ref[side, layout.half + 1 :, :] = low_ref[body + 1 :, :]


def own_place(me):
    return ((me >> 1) & 1) | ((me & 1) << 1)


def span(place, rows):
    return pl.ds(pl.multiple_of(place * rows, LANES), rows)


def place_here():
    return lax.axis_index("blk"), lax.axis_index("rows") & 1


def turn_kernel(*refs):
    blocks, (rows_ref, columns_ref) = refs[:-2], refs[-2:]
    rows, width = blocks[0].shape
    own = own_place(place_here()[0])
    for part, block_ref in enumerate(blocks):
        block = block_ref[...]
        rows_ref[span(part ^ own, rows), :width] = block
        rows_ref[span(part ^ own, rows), width:] = block[:, : rows_ref.shape[1] - width]
        columns_ref[:, span(part ^ own, rows)] = block.T.astype(jnp.float32)


def give_kernel(offsets, normalizer, layout, *refs):
    scores, (rows_ref, columns_ref), refs = refs[:4], refs[4:6], refs[6:]
    resp_ref, low_ref, here_ref, *outs, message_ref = refs
    comps, rows = here_ref.shape
    me, flip = place_here()
    own = own_place(me)
    index = lax.broadcasted_iota(jnp.int32, (comps, 4 * rows), 0)
    table = jnp.zeros((comps, 4 * rows), jnp.float32)
    for source, score_ref in enumerate(scores):
        turn = ((source & 1) << 1) | (source >> 1)
        for b in range(score_ref.shape[0]):
            pieces = [score_ref[b : b + 1, (part ^ turn) * rows : ((part ^ turn) + 1) * rows] for part in range(4)]
            table = jnp.where(index == (me ^ (4 * b + source)), jnp.concatenate(pieces, axis=1), table)
    weights = softmax(table)
    here_ref[...] = weights[:, :rows]
    for part in range(4):
        resp_ref[:, span(part ^ own, rows)] = weights[:, part * rows : (part + 1) * rows]
    weights = resp_ref[...]
    high = weights.astype(jnp.bfloat16).astype(jnp.float32)
    rest = weights - high
    middle = rest.astype(jnp.bfloat16).astype(jnp.float32)
    pieces = [high, middle, rest - middle]
    if 3 * comps % 16:
        pieces.append(jnp.zeros((-3 * comps % 16, 4 * rows), jnp.float32))
    stacked = jnp.concatenate(pieces, axis=0).astype(jnp.bfloat16)
    totals, products = [], {}
    for offset in offsets:
        total, product = moment(weights, me ^ offset, rows_ref, columns_ref, layout, None if products else stacked)
        totals.append(total)
        products = products or product
    product = jnp.concatenate([products[b] for b in range(layout.parts)], axis=1)
    first = (product[:comps] + (product[comps : 2 * comps] + product[2 * comps : 3 * comps])) * normalizer
    count = jnp.sum(weights, axis=1, keepdims=True) * normalizer
    exponent = exponent_of(jnp.max(jnp.abs(first), keepdims=True))
    first = first * power(-exponent)
    body = low_ref.shape[0] - HEAD
    low_ref[...] = jnp.zeros_like(low_ref)
    for a in range(layout.parts):
        low_ref[a * comps : (a + 1) * comps, :] = first[:, a * LANES : (a + 1) * LANES]
    at = layout.parts * comps
    low_ref[at : at + comps, :] = jnp.broadcast_to(count, (comps, LANES))
    low_ref[body:, :] = jnp.broadcast_to(exponent, (HEAD, LANES))
    for at, total in enumerate(totals):
        store_second(total, normalizer, layout, message_ref, 0)
        store_low(low_ref, layout, message_ref, 0)
        part_ways(message_ref, flip, outs[2 * at : 2 * at + 2])


def keep_kernel(normalizer, layout, resp_ref, low_ref, rows_ref, columns_ref, *refs):
    outs, message_ref = refs[:2], refs[2]
    me, flip = place_here()
    store_second(moment(resp_ref[...], me, rows_ref, columns_ref, layout)[0], normalizer, layout, message_ref, 0)
    store_low(low_ref, layout, message_ref, 0)
    part_ways(message_ref, flip, outs)


def tree(values):
    while len(values) > 1:
        values = [values[i] + values[i + 1] for i in range(0, len(values), 2)]
    return values[0]


def decoded_sum(refs, side, layout):
    row = lax.broadcasted_iota(jnp.int32, (layout.half, LANES), 0) + side * layout.half
    is_second, is_first = row < layout.firsts, row < layout.counts

    def at_rows(second, first):
        return jnp.where(is_second, power(second), jnp.where(is_first, power(first), 1.0))

    seconds = [r[layout.half : layout.half + 1, :] for r in refs]
    firsts = [r[layout.half + 1 : layout.half + 2, :] for r in refs]
    total = tree([r[: layout.half, :] * at_rows(s, f) for r, s, f in zip(refs, seconds, firsts, strict=True)])
    return total, seconds, firsts, at_rows


def highest(values):
    return values[0] if len(values) == 1 else jnp.maximum(values[0], highest(values[1:]))


def combine_kernel(layout, *refs):
    refs, out_ref = refs[:-1], refs[-1]
    total, seconds, firsts, at_rows = decoded_sum(refs, place_here()[1], layout)
    grow = float((len(refs) - 1).bit_length())
    second, first = highest(seconds) + grow, highest(firsts) + grow
    out_ref[: layout.half, :] = total * at_rows(-second, -first)
    out_ref[layout.half :, :] = jnp.broadcast_to(first, (HEAD, LANES))
    out_ref[layout.half : layout.half + 1, :] = second


def finish_kernel(layout, count, *refs):
    mine, others = refs[:count], refs[count : 2 * count]
    second_ref, first_ref, count_ref, table_ref = refs[2 * count :]
    side = place_here()[1]
    for part, messages in ((0, mine), (1, others)):
        total, _, _, _ = decoded_sum(messages, side ^ part, layout)
        table_ref[pl.ds(pl.multiple_of((side ^ part) * layout.half, 8), layout.half), :] = total
    parts, comps = layout.parts, layout.comps
    i, j = pair_masks()

    def place(a, b, block):
        second_ref[a * LANES : (a + 1) * LANES, b * LANES : (b + 1) * LANES] = block

    at = 0
    for a, b in layout.pairs:
        block = table_ref[at : at + LANES, :]
        place(a, b, block)
        place(b, a, block.T)
        at += LANES
    lines = [table_ref[layout.diagonals + a : layout.diagonals + a + 1, :] for a in range(parts)]
    for a in range(0, parts - 1, 2):
        block = table_ref[at : at + LANES, :]
        turned = block.T
        place(a, a, jnp.where(i <= j, block, turned))
        place(a + 1, a + 1, jnp.where(i == j, lines[a + 1], jnp.where(i > j, block, turned)))
        at += LANES
    if parts % 2:
        half = LANES // 2
        block = table_ref[at : at + half, :]
        upper = jnp.where((i <= j)[:half], block, 0.0)
        lower = pltpu.roll(jnp.where((i > j)[:half], block, 0.0), half, 1)
        whole = jnp.concatenate([upper, lower], axis=0)
        place(parts - 1, parts - 1, jnp.where(i == j, lines[-1], whole + whole.T))
    at = layout.firsts
    for a in range(parts):
        first_ref[:, a * LANES : (a + 1) * LANES] = table_ref[at : at + comps, :]
        at += comps
    count_ref[...] = table_ref[at : at + comps, :].T[0:1, :]


def call(kernel, out_shape, args, flops, scratch=()):
    specs = [pl.BlockSpec(memory_space=pltpu.VMEM)] * len(args)
    moved = sum(a.size * a.dtype.itemsize for a in args) + sum(
        o.size * o.dtype.itemsize for o in jax.tree.leaves(out_shape)
    )
    return pl.pallas_call(
        kernel,
        out_shape=out_shape,
        in_specs=specs,
        out_specs=jax.tree.map(lambda _: pl.BlockSpec(memory_space=pltpu.VMEM), out_shape),
        scratch_shapes=list(scratch),
        compiler_params=pltpu.CompilerParams(vmem_limit_bytes=VMEM_LIMIT),
        cost_estimate=pl.CostEstimate(flops=flops, bytes_accessed=moved, transcendentals=0),
    )(*args)


def solution(mesh):
    n_blk, n_rows = mesh.shape["blk"], mesh.shape["rows"]
    groups = n_blk // 4

    def hop(value, blk, rows):
        if rows == 0:
            return lax.ppermute(value, "blk", [(i, i ^ blk) for i in range(n_blk)])
        if blk == 0:
            return lax.ppermute(value, "rows", [(i, i ^ rows) for i in range(n_rows)])
        pairs = [
            (i * n_rows + j, (i ^ blk) * n_rows + (j ^ rows)) for i in range(n_blk) for j in range(n_rows)
        ]
        return lax.ppermute(value, ("blk", "rows"), pairs)

    def shards(embeddings, factors, centres, log_prior):
        rows, width = embeddings.shape
        comps = factors.shape[0] * n_blk
        normalizer = comps / (rows * n_blk * n_rows)
        layout = Layout(width, comps)
        low_rows = 2 * layout.half - layout.firsts + HEAD

        near = hop(embeddings, 2, 0)
        matrix = factors.reshape(width, width)
        tail = jnp.concatenate(
            [
                centres,
                jnp.broadcast_to(log_prior[:, None], (1, width)),
                jnp.zeros((TAIL - 2, width), jnp.bfloat16),
            ],
            axis=0,
        )
        core = hop(embeddings, 1, 0)
        matrices = [hop(matrix, 4 * b, 0) for b in range(1, groups)]
        tails = [hop(tail, 4 * b, 0) for b in range(1, groups)]
        flops = 2 * rows * width * width
        line = lambda count, lanes: jax.ShapeDtypeStruct((count, lanes * rows), jnp.float32)
        turned = jax.ShapeDtypeStruct((width, width), jnp.bfloat16)
        own_scores, own_turned = call(
            own_kernel, (line(1, 1), turned), (embeddings, matrix, tail), flops
        )
        near, matrices, tails, own_scores, core = lax.optimization_barrier((near, matrices, tails, own_scores, core))
        far = hop(near, 1, 0)
        tails = [tail] + tails
        most_scores, other_turned = call(
            lambda *refs: near_kernel(groups, *refs),
            (line(groups, 3), jax.ShapeDtypeStruct((groups - 1, width, width), jnp.bfloat16)),
            (embeddings, near, core, own_scores, own_turned, *tails, *matrices),
            (3 * groups - 2) * flops,
        )
        scores = call(
            lambda *refs: far_kernel(groups, *refs),
            line(groups, 4),
            (far, most_scores, own_turned, other_turned, *tails),
            groups * flops,
        )
        scores, far = lax.optimization_barrier((scores, far))
        blocks = (embeddings, near, core, far)
        both = call(
            turn_kernel,
            (
                jax.ShapeDtypeStruct((4 * rows, width + layout.parts // 2 * LANES), jnp.bfloat16),
                jax.ShapeDtypeStruct((width, 4 * rows), jnp.float32),
            ),
            blocks,
            0,
        )
        near_scores = hop(scores, 2, 0)
        core_scores = hop(scores, 1, 0)
        far_scores = hop(near_scores, 1, 0)

        sent = jax.ShapeDtypeStruct((layout.rows, LANES), jnp.float32)
        whole = pltpu.VMEM((2, layout.rows, LANES), jnp.float32)
        flops = 4 * 4 * rows * width * width
        resp, low, here, *given = call(
            lambda *refs: give_kernel([4 * b for b in range(1, groups)], normalizer, layout, *refs),
            (
                jax.ShapeDtypeStruct((comps, 4 * rows), jnp.float32),
                jax.ShapeDtypeStruct((low_rows, LANES), jnp.float32),
                jax.ShapeDtypeStruct((comps, rows), jnp.float32),
                *[sent] * (2 * groups - 2),
            ),
            (scores, core_scores, near_scores, far_scores, *both),
            flops * (groups - 1),
            [whole],
        )
        received = {}
        for b in range(1, groups):
            for z in (1, 0):
                received[b, z] = hop(given[2 * b - 2 + z].astype(jnp.float16), 4 * b, z)
        kept = call(
            lambda *refs: keep_kernel(normalizer, layout, *refs),
            (sent, sent),
            (resp, low, *both),
            flops,
            [whole],
        )
        received[0, 0] = lax.optimization_barrier(kept[0].astype(jnp.float16))
        received[0, 1] = hop(kept[1].astype(jnp.float16), 0, 1)
        for b in range(1, groups):
            received[b, 0], received[b, 1] = lax.optimization_barrier((received[b, 0], received[b, 1]))
        wide = {key: value.astype(jnp.float32) for key, value in received.items()}
        same = [wide[b, 0] for b in range(groups)]
        other = [wide[b, 1] for b in range(1, groups)]
        summed = call(
            lambda *refs: combine_kernel(layout, *refs), sent, (*same, wide[0, 1], *other), 0
        )
        summed = lax.optimization_barrier(summed.astype(jnp.float16))
        bit = 2
        while 2 * bit < n_rows:
            messages = [m.astype(jnp.float32) for m in (summed, hop(summed, 0, bit))]
            summed = call(
                lambda *refs: combine_kernel(layout, *refs), sent, messages, 0
            )
            summed = lax.optimization_barrier(summed.astype(jnp.float16))
            bit *= 2
        last = [0, bit] if bit < n_rows else [0]
        arrived = {z: hop(summed, 0, z) for z in (last[-1], last[-1] ^ 1, 1)}
        if len(last) > 1:
            arrived[bit], arrived[bit ^ 1] = lax.optimization_barrier((arrived[bit], arrived[bit ^ 1]))
        arrived[0] = summed
        mine = [arrived[z] for z in last]
        others = [arrived[z ^ 1] for z in last]
        second, first, count = call(
            lambda *refs: finish_kernel(layout, len(last), *refs),
            (
                jax.ShapeDtypeStruct((width, width), jnp.float32),
                jax.ShapeDtypeStruct((comps, width), jnp.float32),
                jax.ShapeDtypeStruct((1, comps), jnp.float32),
            ),
            [m.astype(jnp.float32) for m in mine + others],
            0,
            [pltpu.VMEM((2 * layout.half, LANES), jnp.float32)],
        )
        return here, count.reshape(comps), first, second.reshape(1, width, width)

    in_specs = (P(("blk", "rows"), None), P("blk", None, None), P("blk", None), P("blk"))
    out_specs = (P(None, ("blk", "rows")), P(), P(), P("blk", None, None))
    return jax.shard_map(shards, mesh=mesh, in_specs=in_specs, out_specs=out_specs, check_vma=False)
```

```python
import jax
import jax.numpy as jnp
from jax import lax
from jax.experimental import pallas as pl
from jax.experimental.pallas import tpu as pltpu
from jax.sharding import PartitionSpec as P

half_temper = 0.05
LANES = 128
TAIL = 16
HEAD = 8
VMEM_LIMIT = 40 * 1024 * 1024
NT = (((1,), (1,)), ((), ()))


def split_two(value):
    high = value.astype(jnp.bfloat16)
    low = (value - high.astype(jnp.float32)).astype(jnp.bfloat16)
    return high, low


def power(exponent):
    whole = exponent.astype(jnp.int32)
    size = jnp.abs(whole)
    result = jnp.ones(exponent.shape, jnp.float32)
    for bit in range(7):
        factor = jnp.where(whole < 0, 0.5 ** (1 << bit), 2.0 ** (1 << bit))
        result = result * jnp.where((size >> bit) & 1 == 1, factor, 1.0)
    return result


def exponent_of(largest):
    bits = jnp.ceil(jnp.log(jnp.maximum(largest, 1e-35)) * 1.4426950408889634) - 12.0
    return jnp.clip(bits, -110.0, 110.0)


def score_rows(turned, tail, rows_ref):
    whitened = lax.dot_general(turned, rows_ref[...], NT, preferred_element_type=jnp.float32)
    whitened = whitened - tail.T[:, 0:1]
    return tail[1:2, 0:1] - half_temper * jnp.sum(whitened * whitened, axis=0, keepdims=True)


def own_kernel(own_ref, matrix_ref, tail_ref, out_ref, turned_ref):
    turned_ref[...] = matrix_ref[...].T
    out_ref[...] = score_rows(turned_ref[...], tail_ref[...].astype(jnp.float32), own_ref)


def near_kernel(groups, own_ref, near_ref, core_ref, done_ref, turned_ref, *refs):
    tails, matrices, (out_ref, others_ref) = refs[:groups], refs[groups : 2 * groups - 1], refs[2 * groups - 1 :]
    rows = own_ref.shape[0]
    for b in range(groups):
        if b:
            others_ref[b - 1] = matrices[b - 1][...].T
        turned = others_ref[b - 1] if b else turned_ref[...]
        tail = tails[b][...].astype(jnp.float32)
        for part, rows_ref in enumerate((own_ref, near_ref, core_ref)):
            if b == 0 and part == 0:
                line = done_ref[...]
            else:
                line = score_rows(turned, tail, rows_ref)
            out_ref[b : b + 1, part * rows : (part + 1) * rows] = line


def far_kernel(groups, far_ref, done_ref, turned_ref, others_ref, *refs):
    tails, out_ref = refs[:groups], refs[groups]
    rows = far_ref.shape[0]
    out_ref[:, : 3 * rows] = done_ref[...]
    for b in range(groups):
        tail = tails[b][...].astype(jnp.float32)
        turned = others_ref[b - 1] if b else turned_ref[...]
        out_ref[b : b + 1, 3 * rows :] = score_rows(turned, tail, far_ref)


def softmax(scores):
    peak = jnp.max(scores, axis=0, keepdims=True)
    unnorm = jnp.exp(scores - peak)
    return unnorm / jnp.sum(unnorm, axis=0, keepdims=True)


def band_pairs(parts):
    return [[(a + d) % parts for d in range(parts // 2 + (parts % 2 or a < parts // 2))] for a in range(parts)]


def moment(weights, component, rows_ref, columns_ref, layout, extra=None):
    picked = lax.broadcasted_iota(jnp.int32, weights.shape, 0) == component
    row = jnp.sum(jnp.where(picked, weights, 0.0), axis=0, keepdims=True)
    blocks, products = {}, {}
    for a, bands in enumerate(band_pairs(layout.parts)):
        left = list(split_two(columns_ref[a * LANES : (a + 1) * LANES, :] * row))
        adds = extra is not None and any(b not in products for b in bands)
        if adds:
            left.append(extra)
        both = jnp.dot(
            jnp.concatenate(left, axis=0),
            rows_ref[:, a * LANES : (a + len(bands)) * LANES],
            preferred_element_type=jnp.float32,
        )
        for d, b in enumerate(bands):
            part = both[:, d * LANES : (d + 1) * LANES]
            blocks[a, b] = part[:LANES] + part[LANES : 2 * LANES]
            if adds:
                products[b] = part[2 * LANES :]
    return blocks, products


def pair_masks():
    i = lax.broadcasted_iota(jnp.int32, (LANES, LANES), 0)
    j = lax.broadcasted_iota(jnp.int32, (LANES, LANES), 1)
    return i, j


class Layout:
    def __init__(self, width, comps):
        self.parts = width // LANES
        self.comps = comps
        self.pairs = [(a, b) for a, bands in enumerate(band_pairs(self.parts)) for b in bands[1:]]
        off = self.parts * (self.parts - 1) // 2 * LANES
        folded = self.parts // 2 * LANES + self.parts % 2 * (LANES // 2)
        self.diagonals = off + folded
        self.firsts = self.diagonals + -(-self.parts // 8) * 8
        self.counts = self.firsts + self.parts * comps
        self.half = -(-(self.counts + comps) // 16) * 8
        self.rows = self.half + HEAD

    def write(self, outs, at, value):
        done = 0
        while done < value.shape[0]:
            side, row = divmod(at + done, self.half)
            count = min(value.shape[0] - done, self.half - row)
            outs[side][row : row + count, :] = value[done : done + count]
            done += count


def store_second(blocks, normalizer, layout, outs):
    parts = layout.parts
    i, j = pair_masks()
    lines = [jnp.sum(jnp.where(i == j, blocks[a, a], 0.0), axis=0, keepdims=True) for a in range(parts)]
    largest = jnp.max(highest(lines), keepdims=True)
    exponent = exponent_of(largest * normalizer)
    factor = normalizer * power(-exponent)
    at = 0
    for a, b in layout.pairs:
        layout.write(outs, at, blocks[a, b] * factor)
        at += LANES
    diagonal = [blocks[a, a] * factor for a in range(parts)]
    for a in range(0, parts - 1, 2):
        layout.write(outs, at, jnp.where(i <= j, diagonal[a], diagonal[a + 1]))
        at += LANES
    if parts % 2:
        half = LANES // 2
        lower = pltpu.roll(diagonal[-1][half:], half, 1)
        layout.write(outs, at, jnp.where(i <= j, diagonal[-1], 0.0)[:half] + jnp.where((i > j)[:half], lower, 0.0))
        at += half
    lines = [line * factor for line in lines]
    lines += [jnp.zeros((1, LANES), jnp.float32)] * (layout.firsts - at - parts)
    layout.write(outs, at, jnp.concatenate(lines, axis=0))
    for side in range(2):
        outs[side][layout.half : layout.half + 1, :] = jnp.broadcast_to(exponent, (1, LANES))


def store_low(low_ref, layout, outs):
    body = low_ref.shape[0] - HEAD
    layout.write(outs, layout.firsts, low_ref[:body, :])
    for side in range(2):
        outs[side][layout.half + 1 :, :] = low_ref[body + 1 :, :]


def own_place(me):
    return ((me >> 1) & 1) | ((me & 1) << 1)


def span(place, rows):
    return pl.ds(pl.multiple_of(place * rows, LANES), rows)


def place_here():
    return lax.axis_index("blk"), lax.axis_index("rows") & 1


def turn_kernel(*refs):
    blocks, (rows_ref, columns_ref) = refs[:-2], refs[-2:]
    rows, width = blocks[0].shape
    own = own_place(place_here()[0])
    for part, block_ref in enumerate(blocks):
        block = block_ref[...]
        rows_ref[span(part ^ own, rows), :width] = block
        rows_ref[span(part ^ own, rows), width:] = block[:, : rows_ref.shape[1] - width]
        columns_ref[:, span(part ^ own, rows)] = block.T.astype(jnp.float32)


def give_kernel(offsets, normalizer, layout, *refs):
    scores, (rows_ref, columns_ref), refs = refs[:4], refs[4:6], refs[6:]
    resp_ref, low_ref, here_ref, *outs = refs
    comps, rows = here_ref.shape
    me, _ = place_here()
    own = own_place(me)
    index = lax.broadcasted_iota(jnp.int32, (comps, 4 * rows), 0)
    table = jnp.zeros((comps, 4 * rows), jnp.float32)
    for source, score_ref in enumerate(scores):
        turn = ((source & 1) << 1) | (source >> 1)
        for b in range(score_ref.shape[0]):
            pieces = [score_ref[b : b + 1, (part ^ turn) * rows : ((part ^ turn) + 1) * rows] for part in range(4)]
            table = jnp.where(index == (me ^ (4 * b + source)), jnp.concatenate(pieces, axis=1), table)
    weights = softmax(table)
    here_ref[...] = weights[:, :rows]
    for part in range(4):
        resp_ref[:, span(part ^ own, rows)] = weights[:, part * rows : (part + 1) * rows]
    weights = resp_ref[...]
    high = weights.astype(jnp.bfloat16).astype(jnp.float32)
    rest = weights - high
    middle = rest.astype(jnp.bfloat16).astype(jnp.float32)
    pieces = [high, middle, rest - middle]
    if 3 * comps % 16:
        pieces.append(jnp.zeros((-3 * comps % 16, 4 * rows), jnp.float32))
    stacked = jnp.concatenate(pieces, axis=0).astype(jnp.bfloat16)
    totals, products = [], {}
    for offset in offsets:
        total, product = moment(weights, me ^ offset, rows_ref, columns_ref, layout, None if products else stacked)
        totals.append(total)
        products = products or product
    product = jnp.concatenate([products[b] for b in range(layout.parts)], axis=1)
    first = (product[:comps] + (product[comps : 2 * comps] + product[2 * comps : 3 * comps])) * normalizer
    count = jnp.sum(weights, axis=1, keepdims=True) * normalizer
    exponent = exponent_of(jnp.max(jnp.abs(first), keepdims=True))
    first = first * power(-exponent)
    body = low_ref.shape[0] - HEAD
    low_ref[...] = jnp.zeros_like(low_ref)
    for a in range(layout.parts):
        low_ref[a * comps : (a + 1) * comps, :] = first[:, a * LANES : (a + 1) * LANES]
    at = layout.parts * comps
    low_ref[at : at + comps, :] = jnp.broadcast_to(count, (comps, LANES))
    low_ref[body:, :] = jnp.broadcast_to(exponent, (HEAD, LANES))
    for at, total in enumerate(totals):
        store_second(total, normalizer, layout, outs[2 * at : 2 * at + 2])
        store_low(low_ref, layout, outs[2 * at : 2 * at + 2])


def keep_kernel(normalizer, layout, resp_ref, low_ref, rows_ref, columns_ref, *refs):
    outs = refs
    me, _ = place_here()
    store_second(moment(resp_ref[...], me, rows_ref, columns_ref, layout)[0], normalizer, layout, outs)
    store_low(low_ref, layout, outs)


def tree(values):
    while len(values) > 1:
        values = [values[i] + values[i + 1] for i in range(0, len(values), 2)]
    return values[0]


def decoded_sum(refs, side, layout):
    row = lax.broadcasted_iota(jnp.int32, (layout.half, LANES), 0) + side * layout.half
    is_second, is_first = row < layout.firsts, row < layout.counts

    def at_rows(second, first):
        return jnp.where(is_second, power(second), jnp.where(is_first, power(first), 1.0))

    seconds = [r[layout.half : layout.half + 1, :] for r in refs]
    firsts = [r[layout.half + 1 : layout.half + 2, :] for r in refs]
    total = tree([r[: layout.half, :] * at_rows(s, f) for r, s, f in zip(refs, seconds, firsts, strict=True)])
    return total, seconds, firsts, at_rows


def highest(values):
    return values[0] if len(values) == 1 else jnp.maximum(values[0], highest(values[1:]))


def combine_kernel(layout, *refs):
    refs, out_ref = refs[:-1], refs[-1]
    total, seconds, firsts, at_rows = decoded_sum(refs, place_here()[1], layout)
    grow = float((len(refs) - 1).bit_length())
    second, first = highest(seconds) + grow, highest(firsts) + grow
    out_ref[: layout.half, :] = total * at_rows(-second, -first)
    out_ref[layout.half :, :] = jnp.broadcast_to(first, (HEAD, LANES))
    out_ref[layout.half : layout.half + 1, :] = second


def finish_kernel(layout, count, *refs):
    mine, others = refs[:count], refs[count : 2 * count]
    second_ref, first_ref, count_ref, table_ref = refs[2 * count :]
    side = place_here()[1]
    for part, messages in ((0, mine), (1, others)):
        total, _, _, _ = decoded_sum(messages, side ^ part, layout)
        table_ref[pl.ds(pl.multiple_of((side ^ part) * layout.half, 8), layout.half), :] = total
    parts, comps = layout.parts, layout.comps
    i, j = pair_masks()

    def place(a, b, block):
        second_ref[a * LANES : (a + 1) * LANES, b * LANES : (b + 1) * LANES] = block

    at = 0
    for a, b in layout.pairs:
        block = table_ref[at : at + LANES, :]
        place(a, b, block)
        place(b, a, block.T)
        at += LANES
    lines = [table_ref[layout.diagonals + a : layout.diagonals + a + 1, :] for a in range(parts)]
    for a in range(0, parts - 1, 2):
        block = table_ref[at : at + LANES, :]
        turned = block.T
        place(a, a, jnp.where(i <= j, block, turned))
        place(a + 1, a + 1, jnp.where(i == j, lines[a + 1], jnp.where(i > j, block, turned)))
        at += LANES
    if parts % 2:
        half = LANES // 2
        block = table_ref[at : at + half, :]
        upper = jnp.where((i <= j)[:half], block, 0.0)
        lower = pltpu.roll(jnp.where((i > j)[:half], block, 0.0), half, 1)
        whole = jnp.concatenate([upper, lower], axis=0)
        place(parts - 1, parts - 1, jnp.where(i == j, lines[-1], whole + whole.T))
    at = layout.firsts
    for a in range(parts):
        first_ref[:, a * LANES : (a + 1) * LANES] = table_ref[at : at + comps, :]
        at += comps
    count_ref[...] = table_ref[at : at + comps, :].T[0:1, :]


def call(kernel, out_shape, args, flops, scratch=()):
    specs = [pl.BlockSpec(memory_space=pltpu.VMEM)] * len(args)
    moved = sum(a.size * a.dtype.itemsize for a in args) + sum(
        o.size * o.dtype.itemsize for o in jax.tree.leaves(out_shape)
    )
    return pl.pallas_call(
        kernel,
        out_shape=out_shape,
        in_specs=specs,
        out_specs=jax.tree.map(lambda _: pl.BlockSpec(memory_space=pltpu.VMEM), out_shape),
        scratch_shapes=list(scratch),
        compiler_params=pltpu.CompilerParams(vmem_limit_bytes=VMEM_LIMIT),
        cost_estimate=pl.CostEstimate(flops=flops, bytes_accessed=moved, transcendentals=0),
    )(*args)


def solution(mesh):
    n_blk, n_rows = mesh.shape["blk"], mesh.shape["rows"]
    groups = n_blk // 4

    def hop(value, blk, rows):
        if rows == 0:
            return lax.ppermute(value, "blk", [(i, i ^ blk) for i in range(n_blk)])
        if blk == 0:
            return lax.ppermute(value, "rows", [(i, i ^ rows) for i in range(n_rows)])
        pairs = [
            (i * n_rows + j, (i ^ blk) * n_rows + (j ^ rows)) for i in range(n_blk) for j in range(n_rows)
        ]
        return lax.ppermute(value, ("blk", "rows"), pairs)

    def shards(embeddings, factors, centres, log_prior):
        rows, width = embeddings.shape
        comps = factors.shape[0] * n_blk
        normalizer = comps / (rows * n_blk * n_rows)
        layout = Layout(width, comps)
        low_rows = 2 * layout.half - layout.firsts + HEAD

        near = hop(embeddings, 2, 0)
        matrix = factors.reshape(width, width)
        tail = jnp.concatenate(
            [
                centres,
                jnp.broadcast_to(log_prior[:, None], (1, width)),
                jnp.zeros((TAIL - 2, width), jnp.bfloat16),
            ],
            axis=0,
        )
        core = hop(embeddings, 1, 0)
        matrices = [hop(matrix, 4 * b, 0) for b in range(1, groups)]
        tails = [hop(tail, 4 * b, 0) for b in range(1, groups)]
        flops = 2 * rows * width * width
        line = lambda count, lanes: jax.ShapeDtypeStruct((count, lanes * rows), jnp.float32)
        turned = jax.ShapeDtypeStruct((width, width), jnp.bfloat16)
        own_scores, own_turned = call(
            own_kernel, (line(1, 1), turned), (embeddings, matrix, tail), flops
        )
        near, matrices, tails, own_scores, core = lax.optimization_barrier((near, matrices, tails, own_scores, core))
        far = hop(near, 1, 0)
        tails = [tail] + tails
        most_scores, other_turned = call(
            lambda *refs: near_kernel(groups, *refs),
            (line(groups, 3), jax.ShapeDtypeStruct((groups - 1, width, width), jnp.bfloat16)),
            (embeddings, near, core, own_scores, own_turned, *tails, *matrices),
            (3 * groups - 2) * flops,
        )
        scores = call(
            lambda *refs: far_kernel(groups, *refs),
            line(groups, 4),
            (far, most_scores, own_turned, other_turned, *tails),
            groups * flops,
        )
        scores, far = lax.optimization_barrier((scores, far))
        blocks = (embeddings, near, core, far)
        both = call(
            turn_kernel,
            (
                jax.ShapeDtypeStruct((4 * rows, width + layout.parts // 2 * LANES), jnp.bfloat16),
                jax.ShapeDtypeStruct((width, 4 * rows), jnp.float32),
            ),
            blocks,
            0,
        )
        near_scores = hop(scores, 2, 0)
        core_scores = hop(scores, 1, 0)
        far_scores = hop(near_scores, 1, 0)

        sent = jax.ShapeDtypeStruct((layout.rows, LANES), jnp.float32)
        odd = (lax.axis_index("rows") & 1) == 1
        flops = 4 * 4 * rows * width * width
        resp, low, here, *given = call(
            lambda *refs: give_kernel([4 * b for b in range(1, groups)], normalizer, layout, *refs),
            (
                jax.ShapeDtypeStruct((comps, 4 * rows), jnp.float32),
                jax.ShapeDtypeStruct((low_rows, LANES), jnp.float32),
                jax.ShapeDtypeStruct((comps, rows), jnp.float32),
                *[sent] * (2 * groups - 2),
            ),
            (scores, core_scores, near_scores, far_scores, *both),
            flops * (groups - 1),
        )
        received = {}
        for b in range(1, groups):
            for z in (1, 0):
                received[b, z] = hop(jnp.where(odd, given[2 * b - 1 - z], given[2 * b - 2 + z]).astype(jnp.float16), 4 * b, z)
        kept = call(
            lambda *refs: keep_kernel(normalizer, layout, *refs),
            (sent, sent),
            (resp, low, *both),
            flops,
        )
        received[0, 0] = lax.optimization_barrier(jnp.where(odd, kept[1], kept[0]).astype(jnp.float16))
        received[0, 1] = hop(jnp.where(odd, kept[0], kept[1]).astype(jnp.float16), 0, 1)
        for b in range(1, groups):
            received[b, 0], received[b, 1] = lax.optimization_barrier((received[b, 0], received[b, 1]))
        wide = {key: value.astype(jnp.float32) for key, value in received.items()}
        same = [wide[b, 0] for b in range(groups)]
        other = [wide[b, 1] for b in range(1, groups)]
        summed = call(
            lambda *refs: combine_kernel(layout, *refs), sent, (*same, wide[0, 1], *other), 0
        )
        summed = lax.optimization_barrier(summed.astype(jnp.float16))
        bit = 2
        while 2 * bit < n_rows:
            messages = [m.astype(jnp.float32) for m in (summed, hop(summed, 0, bit))]
            summed = call(
                lambda *refs: combine_kernel(layout, *refs), sent, messages, 0
            )
            summed = lax.optimization_barrier(summed.astype(jnp.float16))
            bit *= 2
        last = [0, bit] if bit < n_rows else [0]
        arrived = {z: hop(summed, 0, z) for z in (last[-1], last[-1] ^ 1, 1)}
        if len(last) > 1:
            arrived[bit], arrived[bit ^ 1] = lax.optimization_barrier((arrived[bit], arrived[bit ^ 1]))
        arrived[0] = summed
        mine = [arrived[z] for z in last]
        others = [arrived[z ^ 1] for z in last]
        second, first, count = call(
            lambda *refs: finish_kernel(layout, len(last), *refs),
            (
                jax.ShapeDtypeStruct((width, width), jnp.float32),
                jax.ShapeDtypeStruct((comps, width), jnp.float32),
                jax.ShapeDtypeStruct((1, comps), jnp.float32),
            ),
            [m.astype(jnp.float32) for m in mine + others],
            0,
            [pltpu.VMEM((2 * layout.half, LANES), jnp.float32)],
        )
        return here, count.reshape(comps), first, second.reshape(1, width, width)

    in_specs = (P(("blk", "rows"), None), P("blk", None, None), P("blk", None), P("blk"))
    out_specs = (P(None, ("blk", "rows")), P(), P(), P("blk", None, None))
    return jax.shard_map(shards, mesh=mesh, in_specs=in_specs, out_specs=out_specs, check_vma=False)
```

```python
import jax
import jax.numpy as jnp
from jax import lax
from jax.experimental import pallas as pl
from jax.experimental.pallas import tpu as pltpu
from jax.sharding import PartitionSpec as P

half_temper = 0.05
LANES = 128
TAIL = 16
HEAD = 8
VMEM_LIMIT = 40 * 1024 * 1024
NT = (((1,), (1,)), ((), ()))


def split_two(value):
    high = value.astype(jnp.bfloat16)
    low = (value - high.astype(jnp.float32)).astype(jnp.bfloat16)
    return high, low


def power(exponent):
    whole = exponent.astype(jnp.int32)
    size = jnp.abs(whole)
    result = jnp.ones(exponent.shape, jnp.float32)
    for bit in range(7):
        factor = jnp.where(whole < 0, 0.5 ** (1 << bit), 2.0 ** (1 << bit))
        result = result * jnp.where((size >> bit) & 1 == 1, factor, 1.0)
    return result


def exponent_of(largest):
    bits = jnp.ceil(jnp.log(jnp.maximum(largest, 1e-35)) * 1.4426950408889634) - 12.0
    return jnp.clip(bits, -110.0, 110.0)


def score_rows(turned, tail, rows_ref):
    whitened = lax.dot_general(turned, rows_ref[...], NT, preferred_element_type=jnp.float32)
    whitened = whitened - tail.T[:, 0:1]
    return tail[1:2, 0:1] - half_temper * jnp.sum(whitened * whitened, axis=0, keepdims=True)


def own_kernel(own_ref, matrix_ref, tail_ref, out_ref, turned_ref):
    turned_ref[...] = matrix_ref[...].T
    out_ref[...] = score_rows(turned_ref[...], tail_ref[...].astype(jnp.float32), own_ref)


def near_kernel(groups, own_ref, near_ref, core_ref, done_ref, turned_ref, *refs):
    tails, matrices, (out_ref, others_ref) = refs[:groups], refs[groups : 2 * groups - 1], refs[2 * groups - 1 :]
    rows = own_ref.shape[0]
    for b in range(groups):
        if b:
            others_ref[b - 1] = matrices[b - 1][...].T
        turned = others_ref[b - 1] if b else turned_ref[...]
        tail = tails[b][...].astype(jnp.float32)
        for part, rows_ref in enumerate((own_ref, near_ref, core_ref)):
            if b == 0 and part == 0:
                line = done_ref[...]
            else:
                line = score_rows(turned, tail, rows_ref)
            out_ref[b : b + 1, part * rows : (part + 1) * rows] = line


def far_kernel(groups, far_ref, done_ref, turned_ref, others_ref, *refs):
    tails, out_ref = refs[:groups], refs[groups]
    rows = far_ref.shape[0]
    out_ref[:, : 3 * rows] = done_ref[...]
    for b in range(groups):
        tail = tails[b][...].astype(jnp.float32)
        turned = others_ref[b - 1] if b else turned_ref[...]
        out_ref[b : b + 1, 3 * rows :] = score_rows(turned, tail, far_ref)


def softmax(scores):
    peak = jnp.max(scores, axis=0, keepdims=True)
    unnorm = jnp.exp(scores - peak)
    return unnorm / jnp.sum(unnorm, axis=0, keepdims=True)


def band_pairs(parts):
    return [[(a + d) % parts for d in range(parts // 2 + (parts % 2 or a < parts // 2))] for a in range(parts)]


def moment(weights, component, rows_ref, columns_ref, layout, extra=None):
    picked = lax.broadcasted_iota(jnp.int32, weights.shape, 0) == component
    row = jnp.sum(jnp.where(picked, weights, 0.0), axis=0, keepdims=True)
    blocks, products = {}, {}
    for a, bands in enumerate(band_pairs(layout.parts)):
        left = list(split_two(columns_ref[a * LANES : (a + 1) * LANES, :] * row))
        adds = extra is not None and any(b not in products for b in bands)
        if adds:
            left.append(extra)
        both = jnp.dot(
            jnp.concatenate(left, axis=0),
            rows_ref[:, a * LANES : (a + len(bands)) * LANES],
            preferred_element_type=jnp.float32,
        )
        for d, b in enumerate(bands):
            part = both[:, d * LANES : (d + 1) * LANES]
            blocks[a, b] = part[:LANES] + part[LANES : 2 * LANES]
            if adds:
                products[b] = part[2 * LANES :]
    return blocks, products


def pair_masks():
    i = lax.broadcasted_iota(jnp.int32, (LANES, LANES), 0)
    j = lax.broadcasted_iota(jnp.int32, (LANES, LANES), 1)
    return i, j


class Layout:
    def __init__(self, width, comps):
        self.parts = width // LANES
        self.comps = comps
        self.pairs = [(a, b) for a, bands in enumerate(band_pairs(self.parts)) for b in bands[1:]]
        off = self.parts * (self.parts - 1) // 2 * LANES
        folded = self.parts // 2 * LANES + self.parts % 2 * (LANES // 2)
        self.diagonals = off + folded
        self.firsts = self.diagonals + -(-self.parts // 8) * 8
        self.counts = self.firsts + self.parts * comps
        self.half = -(-(self.counts + comps) // 16) * 8
        self.rows = self.half + HEAD

    def write(self, outs, at, value):
        done = 0
        while done < value.shape[0]:
            side, row = divmod(at + done, self.half)
            count = min(value.shape[0] - done, self.half - row)
            outs[side][row : row + count, :] = value[done : done + count]
            done += count


def store_second(blocks, normalizer, layout, outs):
    parts = layout.parts
    i, j = pair_masks()
    lines = [jnp.sum(jnp.where(i == j, blocks[a, a], 0.0), axis=0, keepdims=True) for a in range(parts)]
    largest = jnp.max(highest(lines), keepdims=True)
    exponent = exponent_of(largest * normalizer)
    factor = normalizer * power(-exponent)
    at = 0
    for a, b in layout.pairs:
        layout.write(outs, at, blocks[a, b] * factor)
        at += LANES
    diagonal = [blocks[a, a] * factor for a in range(parts)]
    for a in range(0, parts - 1, 2):
        layout.write(outs, at, jnp.where(i <= j, diagonal[a], diagonal[a + 1]))
        at += LANES
    if parts % 2:
        half = LANES // 2
        lower = pltpu.roll(diagonal[-1][half:], half, 1)
        layout.write(outs, at, jnp.where(i <= j, diagonal[-1], 0.0)[:half] + jnp.where((i > j)[:half], lower, 0.0))
        at += half
    lines = [line * factor for line in lines]
    lines += [jnp.zeros((1, LANES), jnp.float32)] * (layout.firsts - at - parts)
    layout.write(outs, at, jnp.concatenate(lines, axis=0))
    for side in range(2):
        outs[side][layout.half : layout.half + 1, :] = jnp.broadcast_to(exponent, (1, LANES))


def store_low(low_ref, layout, outs):
    body = low_ref.shape[0] - HEAD
    layout.write(outs, layout.firsts, low_ref[:body, :])
    for side in range(2):
        outs[side][layout.half + 1 :, :] = low_ref[body + 1 :, :]


def own_place(me):
    return ((me >> 1) & 1) | ((me & 1) << 1)


def span(place, rows):
    return pl.ds(pl.multiple_of(place * rows, LANES), rows)


def place_here():
    return lax.axis_index("blk"), lax.axis_index("rows") & 1


def turn_kernel(*refs):
    blocks, (rows_ref, columns_ref) = refs[:-2], refs[-2:]
    rows, width = blocks[0].shape
    own = own_place(place_here()[0])
    for part, block_ref in enumerate(blocks):
        block = block_ref[...]
        rows_ref[span(part ^ own, rows), :width] = block
        rows_ref[span(part ^ own, rows), width:] = block[:, : rows_ref.shape[1] - width]
        columns_ref[:, span(part ^ own, rows)] = block.T.astype(jnp.float32)


def give_kernel(offsets, normalizer, layout, *refs):
    scores, (rows_ref, columns_ref), refs = refs[:4], refs[4:6], refs[6:]
    resp_ref, low_ref, here_ref, *outs = refs
    comps, rows = here_ref.shape
    me, _ = place_here()
    own = own_place(me)
    index = lax.broadcasted_iota(jnp.int32, (comps, 4 * rows), 0)
    table = jnp.zeros((comps, 4 * rows), jnp.float32)
    for source, score_ref in enumerate(scores):
        turn = ((source & 1) << 1) | (source >> 1)
        for b in range(score_ref.shape[0]):
            pieces = [score_ref[b : b + 1, (part ^ turn) * rows : ((part ^ turn) + 1) * rows] for part in range(4)]
            table = jnp.where(index == (me ^ (4 * b + source)), jnp.concatenate(pieces, axis=1), table)
    weights = softmax(table)
    here_ref[...] = weights[:, :rows]
    for part in range(4):
        resp_ref[:, span(part ^ own, rows)] = weights[:, part * rows : (part + 1) * rows]
    weights = resp_ref[...]
    high = weights.astype(jnp.bfloat16).astype(jnp.float32)
    rest = weights - high
    middle = rest.astype(jnp.bfloat16).astype(jnp.float32)
    pieces = [high, middle, rest - middle]
    if 3 * comps % 16:
        pieces.append(jnp.zeros((-3 * comps % 16, 4 * rows), jnp.float32))
    stacked = jnp.concatenate(pieces, axis=0).astype(jnp.bfloat16)
    totals, products = [], {}
    for offset in offsets:
        total, product = moment(weights, me ^ offset, rows_ref, columns_ref, layout, None if products else stacked)
        totals.append(total)
        products = products or product
    product = jnp.concatenate([products[b] for b in range(layout.parts)], axis=1)
    first = (product[:comps] + (product[comps : 2 * comps] + product[2 * comps : 3 * comps])) * normalizer
    count = jnp.sum(weights, axis=1, keepdims=True) * normalizer
    exponent = exponent_of(jnp.max(jnp.abs(first), keepdims=True))
    first = first * power(-exponent)
    body = low_ref.shape[0] - HEAD
    low_ref[...] = jnp.zeros_like(low_ref)
    for a in range(layout.parts):
        low_ref[a * comps : (a + 1) * comps, :] = first[:, a * LANES : (a + 1) * LANES]
    at = layout.parts * comps
    low_ref[at : at + comps, :] = jnp.broadcast_to(count, (comps, LANES))
    low_ref[body:, :] = jnp.broadcast_to(exponent, (HEAD, LANES))
    for at, total in enumerate(totals):
        store_second(total, normalizer, layout, outs[2 * at : 2 * at + 2])
        store_low(low_ref, layout, outs[2 * at : 2 * at + 2])


def keep_kernel(normalizer, layout, resp_ref, low_ref, rows_ref, columns_ref, *refs):
    outs = refs
    me, _ = place_here()
    store_second(moment(resp_ref[...], me, rows_ref, columns_ref, layout)[0], normalizer, layout, outs)
    store_low(low_ref, layout, outs)


def tree(values):
    while len(values) > 1:
        values = [values[i] + values[i + 1] for i in range(0, len(values), 2)]
    return values[0]


def decoded_sum(refs, side, layout):
    row = lax.broadcasted_iota(jnp.int32, (layout.half, LANES), 0) + side * layout.half
    is_second, is_first = row < layout.firsts, row < layout.counts

    def at_rows(second, first):
        return jnp.where(is_second, power(second), jnp.where(is_first, power(first), 1.0))

    seconds = [r[layout.half : layout.half + 1, :] for r in refs]
    firsts = [r[layout.half + 1 : layout.half + 2, :] for r in refs]
    total = tree([r[: layout.half, :] * at_rows(s, f) for r, s, f in zip(refs, seconds, firsts, strict=True)])
    return total, seconds, firsts, at_rows


def highest(values):
    return values[0] if len(values) == 1 else jnp.maximum(values[0], highest(values[1:]))


def combine_kernel(layout, *refs):
    refs, out_ref = refs[:-1], refs[-1]
    total, seconds, firsts, at_rows = decoded_sum(refs, place_here()[1], layout)
    grow = float((len(refs) - 1).bit_length())
    second, first = highest(seconds) + grow, highest(firsts) + grow
    out_ref[: layout.half, :] = total * at_rows(-second, -first)
    out_ref[layout.half :, :] = jnp.broadcast_to(first, (HEAD, LANES))
    out_ref[layout.half : layout.half + 1, :] = second


def finish_kernel(layout, count, *refs):
    mine, others = refs[:count], refs[count : 2 * count]
    second_ref, first_ref, count_ref, table_ref = refs[2 * count :]
    side = place_here()[1]
    for part, messages in ((0, mine), (1, others)):
        total, _, _, _ = decoded_sum(messages, side ^ part, layout)
        table_ref[pl.ds(pl.multiple_of((side ^ part) * layout.half, 8), layout.half), :] = total
    parts, comps = layout.parts, layout.comps
    i, j = pair_masks()

    def place(a, b, block):
        second_ref[a * LANES : (a + 1) * LANES, b * LANES : (b + 1) * LANES] = block

    at = 0
    for a, b in layout.pairs:
        block = table_ref[at : at + LANES, :]
        place(a, b, block)
        place(b, a, block.T)
        at += LANES
    lines = [table_ref[layout.diagonals + a : layout.diagonals + a + 1, :] for a in range(parts)]
    for a in range(0, parts - 1, 2):
        block = table_ref[at : at + LANES, :]
        turned = block.T
        place(a, a, jnp.where(i <= j, block, turned))
        place(a + 1, a + 1, jnp.where(i == j, lines[a + 1], jnp.where(i > j, block, turned)))
        at += LANES
    if parts % 2:
        half = LANES // 2
        block = table_ref[at : at + half, :]
        upper = jnp.where((i <= j)[:half], block, 0.0)
        lower = pltpu.roll(jnp.where((i > j)[:half], block, 0.0), half, 1)
        whole = jnp.concatenate([upper, lower], axis=0)
        place(parts - 1, parts - 1, jnp.where(i == j, lines[-1], whole + whole.T))
    at = layout.firsts
    for a in range(parts):
        first_ref[:, a * LANES : (a + 1) * LANES] = table_ref[at : at + comps, :]
        at += comps
    count_ref[...] = table_ref[at : at + comps, :].T[0:1, :]


def call(kernel, out_shape, args, flops, scratch=()):
    specs = [pl.BlockSpec(memory_space=pltpu.VMEM)] * len(args)
    moved = sum(a.size * a.dtype.itemsize for a in args) + sum(
        o.size * o.dtype.itemsize for o in jax.tree.leaves(out_shape)
    )
    return pl.pallas_call(
        kernel,
        out_shape=out_shape,
        in_specs=specs,
        out_specs=jax.tree.map(lambda _: pl.BlockSpec(memory_space=pltpu.VMEM), out_shape),
        scratch_shapes=list(scratch),
        compiler_params=pltpu.CompilerParams(vmem_limit_bytes=VMEM_LIMIT),
        cost_estimate=pl.CostEstimate(flops=flops, bytes_accessed=moved, transcendentals=0),
    )(*args)


def solution(mesh):
    n_blk, n_rows = mesh.shape["blk"], mesh.shape["rows"]
    groups = n_blk // 4

    def hop(value, blk, rows):
        if rows == 0:
            return lax.ppermute(value, "blk", [(i, i ^ blk) for i in range(n_blk)])
        if blk == 0:
            return lax.ppermute(value, "rows", [(i, i ^ rows) for i in range(n_rows)])
        pairs = [
            (i * n_rows + j, (i ^ blk) * n_rows + (j ^ rows)) for i in range(n_blk) for j in range(n_rows)
        ]
        return lax.ppermute(value, ("blk", "rows"), pairs)

    def shards(embeddings, factors, centres, log_prior):
        rows, width = embeddings.shape
        comps = factors.shape[0] * n_blk
        normalizer = comps / (rows * n_blk * n_rows)
        layout = Layout(width, comps)
        low_rows = 2 * layout.half - layout.firsts + HEAD

        near = hop(embeddings, 2, 0)
        matrix = factors.reshape(width, width)
        tail = jnp.concatenate(
            [
                centres,
                jnp.broadcast_to(log_prior[:, None], (1, width)),
                jnp.zeros((TAIL - 2, width), jnp.bfloat16),
            ],
            axis=0,
        )
        core = hop(embeddings, 1, 0)
        matrices = [hop(matrix, 4 * b, 0) for b in range(1, groups)]
        tails = [hop(tail, 4 * b, 0) for b in range(1, groups)]
        flops = 2 * rows * width * width
        line = lambda count, lanes: jax.ShapeDtypeStruct((count, lanes * rows), jnp.float32)
        turned = jax.ShapeDtypeStruct((width, width), jnp.bfloat16)
        own_scores, own_turned = call(
            own_kernel, (line(1, 1), turned), (embeddings, matrix, tail), flops
        )
        near, matrices, tails, own_scores, core = lax.optimization_barrier((near, matrices, tails, own_scores, core))
        far = hop(near, 1, 0)
        tails = [tail] + tails
        most_scores, other_turned = call(
            lambda *refs: near_kernel(groups, *refs),
            (line(groups, 3), jax.ShapeDtypeStruct((groups - 1, width, width), jnp.bfloat16)),
            (embeddings, near, core, own_scores, own_turned, *tails, *matrices),
            (3 * groups - 2) * flops,
        )
        scores = call(
            lambda *refs: far_kernel(groups, *refs),
            line(groups, 4),
            (far, most_scores, own_turned, other_turned, *tails),
            groups * flops,
        )
        scores, far = lax.optimization_barrier((scores, far))
        blocks = (embeddings, near, core, far)
        both = call(
            turn_kernel,
            (
                jax.ShapeDtypeStruct((4 * rows, width + layout.parts // 2 * LANES), jnp.bfloat16),
                jax.ShapeDtypeStruct((width, 4 * rows), jnp.float32),
            ),
            blocks,
            0,
        )
        near_scores = hop(scores, 2, 0)
        core_scores = hop(scores, 1, 0)
        far_scores = hop(near_scores, 1, 0)

        sent = jax.ShapeDtypeStruct((layout.rows, LANES), jnp.float32)
        odd = (lax.axis_index("rows") & 1) == 1
        flops = 4 * 4 * rows * width * width
        resp, low, here, *given = call(
            lambda *refs: give_kernel([4 * b for b in range(1, groups)], normalizer, layout, *refs),
            (
                jax.ShapeDtypeStruct((comps, 4 * rows), jnp.float32),
                jax.ShapeDtypeStruct((low_rows, LANES), jnp.float32),
                jax.ShapeDtypeStruct((comps, rows), jnp.float32),
                *[sent] * (2 * groups - 2),
            ),
            (scores, core_scores, near_scores, far_scores, *both),
            flops * (groups - 1),
        )
        received = {}
        for b in range(1, groups):
            for z in (0, 1):
                received[b, z] = hop(jnp.where(odd, given[2 * b - 1 - z], given[2 * b - 2 + z]).astype(jnp.float16), 4 * b, z)
        kept = call(
            lambda *refs: keep_kernel(normalizer, layout, *refs),
            (sent, sent),
            (resp, low, *both),
            flops,
        )
        received[0, 0] = lax.optimization_barrier(jnp.where(odd, kept[1], kept[0]).astype(jnp.float16))
        received[0, 1] = hop(jnp.where(odd, kept[0], kept[1]).astype(jnp.float16), 0, 1)
        for b in range(1, groups):
            received[b, 1], received[b, 0] = lax.optimization_barrier((received[b, 1], received[b, 0]))
        wide = {key: value.astype(jnp.float32) for key, value in received.items()}
        same = [wide[b, 0] for b in range(groups)]
        other = [wide[b, 1] for b in range(1, groups)]
        summed = call(
            lambda *refs: combine_kernel(layout, *refs), sent, (*same, wide[0, 1], *other), 0
        )
        summed = lax.optimization_barrier(summed.astype(jnp.float16))
        bit = 2
        while 2 * bit < n_rows:
            messages = [m.astype(jnp.float32) for m in (summed, hop(summed, 0, bit))]
            summed = call(
                lambda *refs: combine_kernel(layout, *refs), sent, messages, 0
            )
            summed = lax.optimization_barrier(summed.astype(jnp.float16))
            bit *= 2
        last = [0, bit] if bit < n_rows else [0]
        arrived = {z: hop(summed, 0, z) for z in (last[-1], last[-1] ^ 1, 1)}
        if len(last) > 1:
            arrived[bit], arrived[bit ^ 1] = lax.optimization_barrier((arrived[bit], arrived[bit ^ 1]))
        arrived[0] = summed
        mine = [arrived[z] for z in last]
        others = [arrived[z ^ 1] for z in last]
        second, first, count = call(
            lambda *refs: finish_kernel(layout, len(last), *refs),
            (
                jax.ShapeDtypeStruct((width, width), jnp.float32),
                jax.ShapeDtypeStruct((comps, width), jnp.float32),
                jax.ShapeDtypeStruct((1, comps), jnp.float32),
            ),
            [m.astype(jnp.float32) for m in mine + others],
            0,
            [pltpu.VMEM((2 * layout.half, LANES), jnp.float32)],
        )
        return here, count.reshape(comps), first, second.reshape(1, width, width)

    in_specs = (P(("blk", "rows"), None), P("blk", None, None), P("blk", None), P("blk"))
    out_specs = (P(None, ("blk", "rows")), P(), P(), P("blk", None, None))
    return jax.shard_map(shards, mesh=mesh, in_specs=in_specs, out_specs=out_specs, check_vma=False)
```
